512 devices in a mesh: trow: 8 (over y), tcol: 8 (over x, z_lo), dp: 8 (over z_hi, core).
Axes of the slice: x: 4, y: 8, z: 8 (z_hi: 4, z_lo: 2; z = z_hi * 2 + z_lo), core: 2. Of those that a mesh axis runs over, the one named last changes fastest.
Arguments:
- embeds: bfloat16 [8192, 1024], P('dp'), may hold values from -6 to 6
- frequencies: bfloat16 [1024, 8192], P(None, ('trow', 'tcol')), may hold values from -0.5 to 0.5
- phases: float32 [8192], P(('trow', 'tcol')), may hold values from -3.140625 to 3.140625
- labels: int32 [8192], P('dp'), may hold values from 0 to 999
- weights: float32 [8192, 1000], P(('tcol', 'dp'), 'trow'), may hold values from -6 to 6
Outputs:
- gram_matrix: float32 [8192, 8192], P(('trow', 'dp'), 'tcol')
- new_weights: float32 [8192, 1000], P(('tcol', 'dp'), 'trow')
The draws below stay inside these ranges and needn't reach their ends.
All inputs are finite; a program needn't handle non-finite values.
Results may differ from the reference program's by a relative error of at most 0.023.
Values may be sent and summed in bfloat16 or wider, within the bound.
A program may use at most 64 MiB of HBM per device.

```python
import jax
import jax.numpy as jnp
from jax import lax

DIN = 1024
F = 8192
C = 1000
ROWS_DEV = 1024
ROWS = 8192
N_DP = 8


def with_ends(array, own_key, smallest, largest):
    place = [jax.random.randint(jax.random.fold_in(own_key, axis), (), 0, length) for axis, length in enumerate(array.shape)]
    widest = array.shape.index(max(array.shape))
    next_to = place[:widest] + [(place[widest] + 1) % array.shape[widest]] + place[widest + 1:]
    return array.at[tuple(place)].set(smallest).at[tuple(next_to)].set(largest)


def steps_of(rng, extent, split, smallest, top_value):
    level, own = 1.0, jax.random.fold_in(rng, 6)
    for position, blocks in split:
        steps = jnp.exp(jax.random.uniform(jax.random.fold_in(own, position), (blocks,), jnp.float32, smallest / len(split), top_value / len(split)))
        level = level * jnp.repeat(steps, extent[position] // blocks).reshape([-1 if axis == position else 1 for axis in range(len(extent))])
    return level


def scatter_about(stream_key, dims, deviation, most, shards=(), kind=jnp.bfloat16):
    gain = steps_of(stream_key, dims, shards, -0.22, 0.18) if shards else 1.0
    values = jax.random.normal(stream_key, dims, jnp.float32) * deviation * gain
    return jnp.minimum(jnp.maximum(values, -most), most).astype(kind)


def setup_inputs(seed: int = 0) -> dict:
    seeds = jax.random.split(jax.random.key(seed), 6)
    return {
        "embeds": scatter_about(seeds[0], (ROWS, DIN), 1.0, 6.0, ((0, 8),)),
        "frequencies": scatter_about(seeds[1], (DIN, F), (DIN // 9) ** -0.5, 0.5, ((1, 64),)),
        "phases": jnp.clip(jax.random.uniform(seeds[2], (F,), jnp.float32, -3.140625, 3.140625), -3.140625, 3.140625),
        "labels": with_ends(jax.random.randint(seeds[3], (ROWS,), 0, C), jax.random.fold_in(seeds[3], 1), 0, C - 1).astype(jnp.int32),
        "weights": scatter_about(seeds[4], (F, C), 1.0, 6.0, ((0, 64), (1, 8)), jnp.float32),
    }


ROOT_TWO = 1.4142135623730951
RIDGE = 0.5
STEP_RATE = 0.5


def featurize(embeds, frequencies, phases):
    angles = jnp.dot(embeds, frequencies, preferred_element_type=jnp.float32) + phases
    return (ROOT_TWO * jnp.cos(angles)).astype(jnp.bfloat16)


def rounded(values):
    return lax.optimization_barrier(values.astype(jnp.bfloat16)).astype(jnp.float32)


def reference(embeds, frequencies, phases, labels, weights):
    features = featurize(embeds, frequencies, phases)
    grouped = features.reshape(N_DP, ROWS_DEV, F)
    group_labels = labels.reshape(N_DP, ROWS_DEV)
    class_ids = jnp.arange(C, dtype=jnp.int32)
    contract = (((0,), (0,)), ((), ()))

    def accumulate(carry, group_item):
        gram_sum, label_sum = carry
        group_rows, labels_here = group_item
        wide_rows = group_rows.astype(jnp.float32)
        gram_part = lax.dot_general(wide_rows, wide_rows, contract, precision=lax.Precision.HIGHEST) / ROWS
        onehot = (labels_here[:, None] == class_ids[None, :]).astype(jnp.float32)
        label_part = lax.dot_general(wide_rows, onehot, contract, precision=lax.Precision.HIGHEST) * (C / ROWS)
        return (gram_sum + rounded(gram_part), label_sum + rounded(label_part)), None

    init = (jnp.zeros((F, F), jnp.float32), jnp.zeros((F, C), jnp.float32))
    (gram_sum, label_sum), unused = lax.scan(accumulate, init, (grouped, group_labels))
    gram_matrix = gram_sum + RIDGE * jnp.eye(F, dtype=jnp.float32)
    curvature = jnp.dot(rounded(gram_matrix), rounded(weights), precision=lax.Precision.HIGHEST)
    diag_vals = jnp.diagonal(gram_matrix)
    new_weights = weights - STEP_RATE * (curvature - label_sum) / diag_vals[:, None]
    return gram_matrix, new_weights
```

```python
import jax
import jax.numpy as jnp
from jax import lax
from jax.experimental import pallas as pl
from jax.experimental.pallas import tpu as pltpu
from jax.sharding import PartitionSpec as P

C = 1000
RIDGE = 0.5
STEP_RATE = 0.5
MESH = pl.DeviceIdType.MESH
F32, BF16 = jnp.float32, jnp.bfloat16
NT = (((1,), (1,)), ((), ()))
NN = (((1,), (0,)), ((), ()))

N = 8
W = 128
ROWS = 1024
DIN = 1024
WIDE = DIN + 128
HALF = W // 2
CLS = 125
TOTAL = 8192
ND = 5
INV_PERIOD = 0.15915494309189535
COS = [
    1.4142135623730951 * q
    for q in (
        0.9999999890754399,
        -19.73920450099313,
        64.93911749956553,
        -85.45013994347214,
        60.16763282514798,
        -25.967602441408868,
        6.528658639370483,
    )
]


def dot(a, b, dims):
    return lax.dot_general(a, b, dims, preferred_element_type=F32)


def rem(a, b):
    return lax.rem(a, jnp.int32(b))


def place(a):
    return rem(a, 2) * 4 + lax.div(a, jnp.int32(2))


def rows(i, size):
    return pl.ds(pl.multiple_of(i * size, size), size)


def kernel(
    e_ref, f_ref, p_ref, l_ref, w_ref, gram_ref, new_ref,
    fl, fr, feat, featr, wpad, wown, wall, ts, tb, st, ulab, us, ub,
    gs, gr, gsum, gb16, ra, rb, cs, rc, xb, xt, gb,
    x_s, x_r, q_s, q_r, z_s, z_r, y_s, y_r, sl_s, sl_r, sr_s, sr_r,
    w_s, w_r, t_s, t_r, a_s, a_r, u_s, u_r, g_s, g_r, ra_s, ra_r, rb_s, rb_r, rc_s, rc_r,
    o_s, o_r, v_s,
):
    r, c, d = lax.axis_index("trow"), lax.axis_index("tcol"), lax.axis_index("dp")
    x, zl = lax.div(c, jnp.int32(2)), rem(c, 2)
    h, k = lax.div(d, jnp.int32(2)), rem(d, 2)
    sib = (r, c, 2 * h + 1 - k)
    mine = rows(k, HALF)
    sends = []

    def copy(src, dst, s, t, dev):
        return pltpu.make_async_remote_copy(
            src_ref=src, dst_ref=dst, send_sem=s, recv_sem=t, device_id=dev, device_id_type=MESH
        )

    def send(*args):
        m = copy(*args)
        m.start()
        sends.append(m)

    def arrived(ref, s, t):
        copy(ref, ref, s, t, sib).wait_recv()

    fl[c, :, :DIN] = f_ref[...].astype(F32).T.astype(BF16)
    ph = jnp.broadcast_to(p_ref[...], (W, W)).T
    hi = ph.astype(BF16)
    rest = ph - hi.astype(F32)
    mid = rest.astype(BF16)
    low = (rest - mid.astype(F32)).astype(BF16)
    lane = lax.broadcasted_iota(jnp.int32, (W, W), 1)
    packed = jnp.where(lane == 0, hi.astype(F32), 0.0)
    packed = jnp.where(lane == 1, mid.astype(F32), packed)
    packed = jnp.where(lane == 2, low.astype(F32), packed)
    fl[c, :, DIN:] = packed.astype(BF16)

    xp, xm = rem(x + 1, 4) * 2 + zl, rem(x + 3, 4) * 2 + zl
    xo = rem(x + 2, 4) * 2 + zl
    other = 1 - 2 * zl
    zdev = (r, c + other, 2 * rem(h + zl - k + 4, 4) + k)
    ydev = (rem(r + 7, N), c, d)
    half = fl.at[c, mine]
    send(half, half, x_s.at[0], x_r.at[0], (r, xp, d))
    send(half, half, x_s.at[1], x_r.at[1], (r, xm, d))
    send(half, fr.at[0, mine], y_s.at[0], y_r.at[0], ydev)
    send(half, half, z_s.at[0], z_r.at[0], zdev)

    wpad[...] = jnp.zeros_like(wpad)
    wpad[:, :CLS] = w_ref[...]
    wown[...] = wpad[...].T.astype(BF16)
    wcols = rows(place(d), W)

    def send_w(i, _):
        there = wall.at[:, wcols]

        @pl.when(jnp.logical_or(r != c, i != d))
        def _():
            copy(wown, there, w_s.at[i], w_r.at[d], (c, r, i)).start()

        return 0

    lax.fori_loop(0, N, send_w, 0)

    @pl.when(r == c)
    def _():
        wall[:, wcols] = wown[...]

    def features(src, store):
        phase = src[:, DIN:].astype(F32)
        phase = phase[:, 0:1] + phase[:, 1:2] + phase[:, 2:3]

        def part(i, _):
            s = rows(i, 256)
            angle = dot(src[:, :DIN], e_ref[s, :], NT) + phase
            t = angle * INV_PERIOD
            t = t - jnp.round(t)
            u = t * t
            v = jnp.full_like(u, COS[-1])
            for q in COS[-2::-1]:
                v = v * u + q
            store(s, v.astype(BF16))
            return 0

        lax.fori_loop(0, ROWS // 256, part, 0)

    def left(j):
        def store(s, v):
            feat[rows(place(j), W), s] = v

        features(fl.at[j], store)

    def right(i):
        def store(s, v):
            featr[i * W : (i + 1) * W, s] = v

        features(fr.at[i - 1], store)

    def to_sib_l(j, i):
        send(fl.at[j, mine], fl.at[j, mine], sl_s.at[i], sl_r.at[i], sib)

    def sib_l(j, i):
        arrived(fl.at[j, rows(1 - k, HALF)], sl_s.at[i], sl_r.at[i])

    def hop_y(i):
        piece = fr.at[i, mine]
        arrived(piece, y_s.at[i], y_r.at[i])
        if i < ND - 2:
            send(piece, fr.at[i + 1, mine], y_s.at[i + 1], y_r.at[i + 1], ydev)
        send(piece, piece, sr_s.at[i], sr_r.at[i], sib)

    def sib_r(i):
        arrived(fr.at[i, rows(1 - k, HALF)], sr_s.at[i], sr_r.at[i])

    left(c)
    featr[0:W, :] = feat[rows(place(c), W), :]

    quarters = (pl.ds(pl.multiple_of(k * HALF, 32), 32), pl.ds(pl.multiple_of(k * HALF + 32, 32), 32))
    for i, (j, on) in enumerate(((xm, xp), (xp, xm))):
        arrived(fl.at[j, mine], x_s.at[i], x_r.at[i])
        send(fl.at[j, quarters[i]], fl.at[j, quarters[i]], q_s.at[i], q_r.at[i], (r, on, d))
        send(fl.at[j, mine], fl.at[j, mine], z_s.at[1 + i], z_r.at[1 + i], zdev)
        to_sib_l(j, i)
    hop_y(0)
    zc = c + other
    arrived(fl.at[zc, mine], z_s.at[0], z_r.at[0])
    to_sib_l(zc, 2)
    for i in range(2):
        arrived(fl.at[xo, quarters[i]], q_s.at[i], q_r.at[i])
    send(fl.at[xo, mine], fl.at[xo, mine], z_s.at[3], z_r.at[3], zdev)
    to_sib_l(xo, 3)
    sib_l(xm, 0)
    left(xm)
    hop_y(1)
    sib_l(xp, 1)
    left(xp)
    for i, j in ((1, xm + other), (2, xp + other)):
        arrived(fl.at[j, mine], z_s.at[i], z_r.at[i])
        to_sib_l(j, 3 + i)
    sib_l(zc, 2)
    left(zc)
    hop_y(2)
    sib_l(xo, 3)
    left(xo)
    arrived(fl.at[xo + other, mine], z_s.at[3], z_r.at[3])
    to_sib_l(xo + other, 6)
    hop_y(3)
    for i, j in ((4, xm + other), (5, xp + other), (6, xo + other)):
        sib_l(j, i)
        left(j)

    def wait_w(i, _):
        @pl.when(jnp.logical_or(r != c, i != d))
        def _():
            arrived(wall.at[:, rows(place(i), W)], w_s.at[i], w_r.at[i])

        return 0

    lax.fori_loop(0, N, wait_w, 0)
    ts[...] = dot(wall[...], feat[...], NN).astype(BF16)

    def send_t(i, _):
        @pl.when(i != r)
        def _():
            copy(ts.at[rows(i, 16)], tb.at[r], t_s.at[i], t_r.at[r], (i, c, d)).start()

        return 0

    lax.fori_loop(0, N, send_t, 0)
    tb[r] = ts[rows(r, 16), :]

    for i in range(1, ND):
        sib_r(i - 1)
        right(i)

    scale = 1.0 / TOTAL
    gs[...] = (dot(feat[rows(1 - k, 512), :], featr[...], NT) * scale).astype(BF16)
    send(gs, gr, g_s.at[0], g_r.at[0], sib)
    gsum[...] = dot(feat[rows(k, 512), :], featr[...], NT) * scale

    def wait_t(i, _):
        @pl.when(i != r)
        def _():
            arrived(tb.at[i], t_s.at[i], t_r.at[i])

        return 0

    lax.fori_loop(0, N, wait_t, 0)
    total = tb[0].astype(F32)
    for i in range(1, N):
        total = total + tb[i].astype(F32)
    st[rows(r, 16), :] = total.astype(BF16)

    def send_a(i, _):
        @pl.when(i != r)
        def _():
            copy(st.at[rows(r, 16)], st.at[rows(r, 16)], a_s.at[i], a_r.at[r], (i, c, d)).start()

        return 0

    lax.fori_loop(0, N, send_a, 0)

    arrived(gr, g_s.at[0], g_r.at[0])
    gsum[...] = gsum[...] + gr[...].astype(F32)
    gb16[...] = gsum[...].astype(BF16)
    hp, hm, ho = rem(h + 1, 4), rem(h + 3, 4), rem(h + 2, 4)
    up, down = (r, c, 2 * hp + k), (r, c, 2 * hm + k)

    def part(i, half):
        return pl.ds(pl.multiple_of(i * W + half * HALF, HALF), HALF)

    send(gb16.at[part(ho, 0)], ra.at[0], ra_s.at[0], ra_r.at[0], up)
    send(gb16.at[part(ho, 1)], ra.at[1], ra_s.at[1], ra_r.at[1], down)
    send(gb16.at[part(hp, 1)], rb.at[0], rb_s.at[0], rb_r.at[0], up)
    send(gb16.at[part(hm, 0)], rb.at[1], rb_s.at[1], rb_r.at[1], down)

    cls = lax.broadcasted_iota(jnp.int32, (W, ROWS), 0)
    onehot = jnp.where(l_ref[...] == cls + c * CLS, 1.0, 0.0).astype(BF16)
    own_f = feat[...].astype(F32)
    diag = jnp.sum(own_f * own_f, axis=1, keepdims=True)
    lane_u = lax.broadcasted_iota(jnp.int32, (N * W, W), 1)
    ulab[...] = jnp.where(lane_u == CLS, diag, -C * dot(feat[...], onehot, NT)) * scale

    for i, (to, dev) in enumerate(((hp, up), (hm, down))):
        arrived(ra.at[i], ra_s.at[i], ra_r.at[i])
        cs[i] = (gsum[part(to, i), :] + ra[i].astype(F32)).astype(BF16)
        send(cs.at[i], rc.at[i], rc_s.at[i], rc_r.at[i], dev)

    def wait_a(i, _):
        @pl.when(i != r)
        def _():
            arrived(st.at[rows(i, 16)], a_s.at[i], a_r.at[i])

        return 0

    lax.fori_loop(0, N, wait_a, 0)
    step = dot(feat[...], st[...], NT) * scale
    us[...] = (jnp.where(lane_u == CLS, 0.0, step) + ulab[...]).astype(BF16)

    def send_u(i, _):
        @pl.when(jnp.logical_or(r != c, i != d))
        def _():
            copy(us.at[rows(place(i), W)], ub.at[d], u_s.at[i], u_r.at[d], (c, r, i)).start()

        return 0

    lax.fori_loop(0, N, send_u, 0)

    @pl.when(r == c)
    def _():
        ub[d] = us[rows(place(d), W), :]

    for i in range(2):
        arrived(rb.at[i], rb_s.at[i], rb_r.at[i])
        arrived(rc.at[i], rc_s.at[i], rc_r.at[i])
    top = gsum[part(h, 0), :] + rc[0].astype(F32) + rb[1].astype(F32)
    low_half = gsum[part(h, 1), :] + rb[0].astype(F32) + rc[1].astype(F32)
    total = jnp.concatenate([top, low_half], axis=0)
    for i in range(ND):
        xb[i] = total[:, i * W : (i + 1) * W].astype(BF16)
        to = rem(r + i, N)

        @pl.when(to != c)
        def _():
            copy(xb.at[i], gb.at[c], o_s.at[i], o_r.at[c], (r, to, d)).start()

        @pl.when(to == c)
        def _():
            gb[c] = xb[i]

        if 0 < i < ND - 1:
            xt[i - 1] = total[:, i * W : (i + 1) * W].T.astype(BF16)
            send(xt.at[i - 1], gb.at[d], v_s.at[i - 1], o_r.at[d], (to, r, c))

    def wait_u(i, _):
        @pl.when(jnp.logical_or(r != c, i != d))
        def _():
            arrived(ub.at[i], u_s.at[i], u_r.at[i])

        return 0

    lax.fori_loop(0, N, wait_u, 0)
    grad = ub[0].astype(F32)
    for i in range(1, N):
        grad = grad + ub[i].astype(F32)
    old = wpad[...]
    diag = grad[:, CLS : CLS + 1] + RIDGE
    new = old - STEP_RATE * (grad + RIDGE * old) / diag
    new_ref[...] = new[:, :CLS]

    delta = rem(c - r + N, N)

    def wait_o(i, _):
        @pl.when(jnp.logical_or(delta >= ND, i != c))
        def _():
            arrived(gb.at[i], o_s.at[0], o_r.at[i])

        return 0

    lax.fori_loop(0, N, wait_o, 0)
    eye = lax.broadcasted_iota(jnp.int32, (W, W), 0) == lane
    for i in range(N):
        ridge = jnp.where(jnp.logical_and(eye, jnp.logical_and(r == c, d == i)), RIDGE, 0.0)
        gram_ref[:, i * W : (i + 1) * W] = gb[i].astype(F32) + ridge

    for m in sends:
        m.wait_send()

    def sent(i, _):
        @pl.when(jnp.logical_or(r != c, i != d))
        def _():
            copy(wown, wown, w_s.at[i], w_r.at[i], sib).wait_send()
            copy(ub.at[0], ub.at[0], u_s.at[i], u_r.at[i], sib).wait_send()

        @pl.when(i != r)
        def _():
            copy(tb.at[0], tb.at[0], t_s.at[i], t_r.at[i], sib).wait_send()
            copy(tb.at[0], tb.at[0], a_s.at[i], a_r.at[i], sib).wait_send()

        return 0

    lax.fori_loop(0, N, sent, 0)
    for i in range(ND):

        @pl.when(rem(r + i, N) != c)
        def _():
            copy(xb.at[i], xb.at[i], o_s.at[i], o_r.at[0], sib).wait_send()


def shards(embeds, frequencies, phases, labels, weights):
    vmem = pl.BlockSpec(memory_space=pltpu.VMEM)
    sem = lambda *n: pltpu.SemaphoreType.DMA(n)
    buffers = [
        ((N, W, WIDE), BF16),
        ((ND - 1, W, WIDE), BF16),
        ((N * W, ROWS), BF16),
        ((ND * W, ROWS), BF16),
        ((W, W), F32),
        ((W, W), BF16),
        ((W, N * W), BF16),
        ((W, ROWS), BF16),
        ((N, 16, ROWS), BF16),
        ((W, ROWS), BF16),
        ((N * W, W), F32),
        ((N * W, W), BF16),
        ((N, W, W), BF16),
        ((4 * W, ND * W), BF16),
        ((4 * W, ND * W), BF16),
        ((4 * W, ND * W), F32),
        ((4 * W, ND * W), BF16),
        ((2, HALF, ND * W), BF16),
        ((2, HALF, ND * W), BF16),
        ((2, HALF, ND * W), BF16),
        ((2, HALF, ND * W), BF16),
        ((ND, W, W), BF16),
        ((ND - 2, W, W), BF16),
        ((N, W, W), BF16),
    ]
    pairs = [2, 2, 4, 4, 7, 4, N, N, N, N, 1, 2, 2, 2]
    sems = [sem(n) for n in pairs for _ in range(2)] + [sem(ND), sem(N), sem(ND - 2)]
    return pl.pallas_call(
        kernel,
        out_shape=(
            jax.ShapeDtypeStruct((W, N * W), F32),
            jax.ShapeDtypeStruct((W, CLS), F32),
        ),
        in_specs=[vmem] * 5,
        out_specs=(vmem, vmem),
        scratch_shapes=[pltpu.VMEM(*b) for b in buffers] + sems,
        compiler_params=pltpu.CompilerParams(
            has_side_effects=True, vmem_limit_bytes=50 * 2**20
        ),
    )(embeds, frequencies, phases.reshape(1, W), labels.reshape(1, ROWS), weights)


def solution(mesh):
    return jax.shard_map(
        shards,
        mesh=mesh,
        in_specs=(
            P("dp", None),
            P(None, ("trow", "tcol")),
            P(("trow", "tcol")),
            P("dp"),
            P(("tcol", "dp"), "trow"),
        ),
        out_specs=(P(("trow", "dp"), "tcol"), P(("tcol", "dp"), "trow")),
        check_vma=False,
    )
```

```python
import jax
import jax.numpy as jnp
from jax import lax
from jax.experimental import pallas as pl
from jax.experimental.pallas import tpu as pltpu
from jax.sharding import PartitionSpec as P

C = 1000
RIDGE = 0.5
STEP_RATE = 0.5
MESH = pl.DeviceIdType.MESH
F32, BF16 = jnp.float32, jnp.bfloat16
NT = (((1,), (1,)), ((), ()))
NN = (((1,), (0,)), ((), ()))

N = 8
W = 128
ROWS = 1024
DIN = 1024
WIDE = DIN + 128
HALF = W // 2
CLS = 125
TOTAL = 8192
ND = 5
GROUPS = (3 * W, 2 * W, W)
INV_PERIOD = 0.15915494309189535
COS = [
    1.4142135623730951 * q
    for q in (
        0.9999999890754399,
        -19.73920450099313,
        64.93911749956553,
        -85.45013994347214,
        60.16763282514798,
        -25.967602441408868,
        6.528658639370483,
    )
]


def dot(a, b, dims):
    return lax.dot_general(a, b, dims, preferred_element_type=F32)


def rem(a, b):
    return lax.rem(a, jnp.int32(b))


def place(a):
    return rem(a, 2) * 4 + lax.div(a, jnp.int32(2))


def rows(i, size):
    return pl.ds(pl.multiple_of(i * size, size), size)


def kernel(
    e_hbm, f_hbm, p_hbm, l_hbm, w_hbm, gram_hbm, new_hbm,
    e_ref, f_ref, p_ref, l_ref, w_ref, gram_ref, new_ref,
    fl, fr, feat, featr, wpad, wown, wall, ts, tb, st, ulab, xb, xt, gb, us, ub, *rest
):
    kinds = ("gs", "gr", "gsum", "gb16", "ra", "rb", "cs", "rc", "sem_s", "sem_r")
    groups = [dict(zip(kinds, rest[i :: len(GROUPS)])) for i in range(len(GROUPS))]
    (
        in_s, out_s, x_s, x_r, q_s, q_r, z_s, z_r, y_s, y_r, sl_s, sl_r, sr_s, sr_r,
        w1_s, w1_r, w2_s, w2_r, w3_s, w3_r, t_s, t_r, a_s, a_r, u_s, u_r, o_s, o_r, v_s,
    ) = rest[len(kinds) * len(GROUPS) :]
    r, c, d = lax.axis_index("trow"), lax.axis_index("tcol"), lax.axis_index("dp")
    x, zl = lax.div(c, jnp.int32(2)), rem(c, 2)
    h, k = lax.div(d, jnp.int32(2)), rem(d, 2)
    other = 1 - 2 * zl
    sib = (r, c, 2 * h + 1 - k)
    flipped = (c, r, d)
    zdev = (r, c + other, 2 * rem(h + zl - k + 4, 4) + k)
    zsrc = (r, c + other, 2 * rem(h + zl + k + 3, 4) + k)
    sends = []

    barrier = pltpu.get_barrier_semaphore()

    def here(*dev):
        pl.semaphore_signal(barrier, inc=1, device_id=dev, device_id_type=MESH)

    def greet(i, _):
        here(rem(r + i, N), c, d)
        here(r, rem(c + i, N), d)
        here(r, c, rem(d + i, N))
        return 0

    lax.fori_loop(1, N, greet, 0)
    here(*zsrc)

    @pl.when(r != c)
    def _():
        here(*flipped)

    behind = rem(r - c + N, N)

    @pl.when(jnp.logical_and(behind >= 1, behind <= ND - 2))
    def _():
        def to_source(i, _):
            here(c, d, i)
            return 0

        lax.fori_loop(0, N, to_source, 0)

    loads = [
        pltpu.make_async_copy(a, b, in_s.at[i])
        for i, (a, b) in enumerate(
            ((f_hbm, f_ref), (p_hbm, p_ref), (w_hbm, w_ref), (l_hbm, l_ref), (e_hbm, e_ref))
        )
    ]
    for m in loads:
        m.start()

    def copy(src, dst, s, t, dev):
        return pltpu.make_async_remote_copy(
            src_ref=src, dst_ref=dst, send_sem=s, recv_sem=t, device_id=dev, device_id_type=MESH
        )

    def send(*args):
        m = copy(*args)
        m.start()
        sends.append(m)

    def arrived(ref, s, t):
        copy(ref, ref, s, t, sib).wait_recv()

    def half(i, core=None):
        return pl.ds(pl.multiple_of(i * W + (k if core is None else core) * HALF, HALF), HALF)

    lane = lax.broadcasted_iota(jnp.int32, (W, W), 1)
    loads[0].wait()
    fl[:W, :DIN] = f_ref[...].astype(F32).T.astype(BF16)
    loads[1].wait()
    ph = jnp.broadcast_to(p_ref[...], (W, W)).T
    hi = ph.astype(BF16)
    left_over = ph - hi.astype(F32)
    mid = left_over.astype(BF16)
    low = (left_over - mid.astype(F32)).astype(BF16)
    packed = jnp.where(lane == 0, hi.astype(F32), 0.0)
    packed = jnp.where(lane == 1, mid.astype(F32), packed)
    packed = jnp.where(lane == 2, low.astype(F32), packed)
    fl[:W, DIN:] = packed.astype(BF16)
    loads[2].wait()
    wpad[...] = jnp.zeros_like(wpad)
    wpad[:, :CLS] = w_ref[...]
    wown[...] = wpad[...].T.astype(BF16)

    pl.semaphore_wait(barrier, 3 * (N - 1) + 1 + ND - 2 + jnp.where(r != c, 1, 0))

    xp, xm, xo = (rem(x + i, 4) * 2 + zl for i in (1, 3, 2))
    slots = [c, xm, xp, xo, c + other, xm + other, xp + other, xo + other]
    ydev = (rem(r + 7, N), c, d)
    own = fl.at[half(0)]
    send(own, fl.at[half(1)], x_s.at[0], x_r.at[0], (r, xp, d))
    send(own, fl.at[half(2)], x_s.at[1], x_r.at[1], (r, xm, d))
    send(own, fr.at[half(0)], y_s.at[0], y_r.at[0], ydev)
    send(own, fl.at[half(4)], z_s.at[0], z_r.at[0], zdev)

    wcols = rows(place(d), W)
    wmine = wall.at[:, wcols]

    @pl.when(r != c)
    def _():
        copy(wown, wmine, w1_s.at[0], w1_r.at[0], flipped).start()

    @pl.when(r == c)
    def _():
        wall[:, wcols] = wown[...]

    def cosines(src, n):
        phase = src[:, DIN:].astype(F32)
        phase = phase[:, 0:1] + phase[:, 1:2] + phase[:, 2:3]
        angle = dot(src[:, :DIN], e_ref[...], NT) + phase
        t = angle * INV_PERIOD
        t = t - jnp.round(t)
        u = t * t
        v = jnp.full_like(u, COS[-1])
        for q in COS[-2::-1]:
            v = v * u + q
        return v.astype(BF16)

    def left(first, n):
        v = cosines(fl.at[first * W : (first + n) * W], n)
        for i in range(n):
            feat[rows(place(slots[first + i]), W), :] = v[i * W : (i + 1) * W]

    def right(first, n):
        featr[(first + 1) * W : (first + 1 + n) * W, :] = cosines(fr.at[first * W : (first + n) * W], n)

    def to_sib(i):
        send(fl.at[half(i)], fl.at[half(i)], sl_s.at[i], sl_r.at[i], sib)

    def to_z(i):
        send(fl.at[half(i)], fl.at[half(4 + i)], z_s.at[i], z_r.at[i], zdev)

    def from_z(i):
        arrived(fl.at[half(4 + i)], z_s.at[i], z_r.at[i])
        to_sib(4 + i)

    def from_sib(*which):
        for i in which:
            arrived(fl.at[half(i, 1 - k)], sl_s.at[i], sl_r.at[i])

    def hop_y(i):
        piece = fr.at[half(i)]
        arrived(piece, y_s.at[i], y_r.at[i])
        if i < ND - 2:
            send(piece, fr.at[half(i + 1)], y_s.at[i + 1], y_r.at[i + 1], ydev)
        send(piece, piece, sr_s.at[i], sr_r.at[i], sib)

    def sib_y(*which):
        for i in which:
            arrived(fr.at[half(i, 1 - k)], sr_s.at[i], sr_r.at[i])

    loads[4].wait()
    left(0, 1)
    featr[0:W, :] = feat[rows(place(c), W), :]

    def quarter(slot, i):
        return fl.at[pl.ds(pl.multiple_of(slot * W + k * HALF + i * 32, 32), 32)]

    for i, (slot, on) in enumerate(((1, xp), (2, xm))):
        arrived(fl.at[half(slot)], x_s.at[i], x_r.at[i])
        send(quarter(slot, i), quarter(3, i), q_s.at[i], q_r.at[i], (r, on, d))
        to_z(slot)
        to_sib(slot)
    hop_y(0)
    from_z(0)

    @pl.when(r != c)
    def _():
        arrived(wmine, w1_s.at[0], w1_r.at[0])

    send(wmine, wmine, w3_s.at[0], w3_r.at[0], sib)
    for i in range(1, 4):
        send(wmine, wmine, w2_s.at[i], w2_r.at[i], (r, c, 2 * rem(h + i, 4) + k))

    from_sib(1, 2)
    left(1, 2)
    hop_y(1)
    for i in range(2):
        arrived(quarter(3, i), q_s.at[i], q_r.at[i])
    to_z(3)
    to_sib(3)
    from_z(1)
    from_z(2)
    for i in range(1, 4):
        piece = wall.at[:, rows(place(2 * rem(h + 4 - i, 4) + k), W)]
        arrived(piece, w2_s.at[i], w2_r.at[i])
        send(piece, piece, w3_s.at[i], w3_r.at[i], sib)
    from_sib(3, 4)
    left(3, 2)
    hop_y(2)
    from_z(3)
    from_sib(5, 6, 7)
    left(5, 3)

    for i in range(4):
        arrived(wall.at[:, rows(place(2 * rem(h + 4 - i, 4) + 1 - k), W)], w3_s.at[i], w3_r.at[i])
    ts[...] = dot(wall[...], feat[...], NN).astype(BF16)
    for i in range(1, N):
        to = rem(r + i, N)
        send(ts.at[rows(to, 16)], tb.at[i], t_s.at[i], t_r.at[i], (to, c, d))
    hop_y(3)

    scale = 1.0 / TOTAL

    def gram_partial(g, first, n):
        cols = featr[first * W : (first + n) * W, :]
        g["gs"][...] = (dot(feat[rows(1 - k, 512), :], cols, NT) * scale).astype(BF16)
        swap(g)
        g["gsum"][...] = dot(feat[rows(k, 512), :], cols, NT) * scale

    def swap(g):
        send(g["gs"], g["gr"], g["sem_s"].at[0], g["sem_r"].at[0], sib)

    hp, hm, ho = rem(h + 1, 4), rem(h + 3, 4), rem(h + 2, 4)
    up, down = (r, c, 2 * hp + k), (r, c, 2 * hm + k)

    def step_one(g):
        arrived(g["gr"], g["sem_s"].at[0], g["sem_r"].at[0])
        g["gsum"][...] = g["gsum"][...] + g["gr"][...].astype(F32)
        g["gb16"][...] = g["gsum"][...].astype(BF16)
        for n, (name, i, at, core, dev) in enumerate(
            (
                ("ra", 0, ho, 0, up),
                ("ra", 1, ho, 1, down),
                ("rb", 0, hp, 1, up),
                ("rb", 1, hm, 0, down),
            )
        ):
            send(g["gb16"].at[half(at, core)], g[name].at[i], g["sem_s"].at[1 + n], g["sem_r"].at[1 + n], dev)

    def step_two(g):
        for i, (at, dev) in enumerate(((hp, up), (hm, down))):
            arrived(g["ra"].at[i], g["sem_s"].at[1 + i], g["sem_r"].at[1 + i])
            g["cs"][i] = (g["gsum"][half(at, i), :] + g["ra"][i].astype(F32)).astype(BF16)
            send(g["cs"].at[i], g["rc"].at[i], g["sem_s"].at[5 + i], g["sem_r"].at[5 + i], dev)

    def step_three(g):
        for i in range(2):
            arrived(g["rb"].at[i], g["sem_s"].at[3 + i], g["sem_r"].at[3 + i])
            arrived(g["rc"].at[i], g["sem_s"].at[5 + i], g["sem_r"].at[5 + i])
        upper = g["gsum"][half(h, 0), :] + g["rc"][0].astype(F32) + g["rb"][1].astype(F32)
        lower = g["gsum"][half(h, 1), :] + g["rb"][0].astype(F32) + g["rc"][1].astype(F32)
        return jnp.concatenate([upper, lower], axis=0)

    def hand_out(g, first, n):
        total = step_three(g)
        for i in range(first, first + n):
            block = total[:, (i - first) * W : (i - first + 1) * W]
            xb[i] = block.astype(BF16)
            to = rem(r + i, N)

            @pl.when(to != c)
            def _():
                copy(xb.at[i], gb.at[c], o_s.at[i], o_r.at[c], (r, to, d)).start()

            @pl.when(to == c)
            def _():
                gb[c] = xb[i]

            if 0 < i < ND - 1:
                xt[i - 1] = block.T.astype(BF16)
                send(xt.at[i - 1], gb.at[d], v_s.at[i - 1], o_r.at[d], (to, r, c))

    sib_y(0, 1)
    right(0, 2)
    gram_partial(groups[0], 0, 3)
    step_one(groups[0])

    total = ts[rows(r, 16), :].astype(F32)
    for i in range(1, N):
        arrived(tb.at[i], t_s.at[i], t_r.at[i])
        total = total + tb[i].astype(F32)
    strip = st.at[rows(r, 16)]
    st[rows(r, 16), :] = total.astype(BF16)
    for i in range(1, N):
        send(strip, strip, a_s.at[i], a_r.at[i], (rem(r + i, N), c, d))

    sib_y(2, 3)
    right(2, 2)
    step_two(groups[0])
    gram_partial(groups[1], 3, 2)
    step_one(groups[1])

    loads[3].wait()
    cls = lax.broadcasted_iota(jnp.int32, (W, ROWS), 0)
    onehot = jnp.where(l_ref[...] == cls + c * CLS, 1.0, 0.0).astype(BF16)
    own_f = feat[...].astype(F32)
    diag = jnp.sum(own_f * own_f, axis=1, keepdims=True)
    lane_u = lax.broadcasted_iota(jnp.int32, (N * W, W), 1)
    ulab[...] = jnp.where(lane_u == CLS, diag, -C * dot(feat[...], onehot, NT)) * scale
    hand_out(groups[0], 0, 3)
    step_two(groups[1])

    for i in range(1, N):
        arrived(st.at[rows(rem(r + N - i, N), 16)], a_s.at[i], a_r.at[i])
    ulab[...] = jnp.where(lane_u == CLS, 0.0, dot(feat[...], st[...], NT) * scale) + ulab[...]
    g = groups[2]
    g["gs"][...] = ulab[rows(1 - k, 512), :].astype(BF16)
    swap(g)
    g["gsum"][...] = ulab[rows(k, 512), :]
    step_one(g)
    hand_out(groups[1], 3, 2)
    step_two(g)

    delta = rem(c - r + N, N)
    eye = lax.broadcasted_iota(jnp.int32, (W, W), 0) == lane

    def gram_block(i, _):
        @pl.when(jnp.logical_or(delta >= ND, i != c))
        def _():
            arrived(gb.at[i], o_s.at[0], o_r.at[i])

        ridge = jnp.where(jnp.logical_and(eye, jnp.logical_and(r == c, d == i)), RIDGE, 0.0)
        gram_ref[i] = gb[i].astype(F32) + ridge
        pltpu.make_async_copy(gram_ref.at[i], gram_hbm.at[:, rows(i, W)], out_s.at[i]).start()
        return 0

    total = step_three(g)
    first = total.astype(BF16).astype(F32)
    second = (total - first)[:, CLS : CLS + 1]
    us[...] = jnp.where(lane == CLS + 1, second, total).astype(BF16)

    @pl.when(r != c)
    def _():
        copy(us, ub, u_s.at[0], u_r.at[0], flipped).start()

    @pl.when(r == c)
    def _():
        ub[...] = us[...]

    lax.fori_loop(0, N, gram_block, 0)

    @pl.when(r != c)
    def _():
        arrived(ub, u_s.at[0], u_r.at[0])

    grad = ub[...].astype(F32)
    old = wpad[...]
    diag = grad[:, CLS : CLS + 1] + grad[:, CLS + 1 : CLS + 2] + RIDGE
    new = old - STEP_RATE * (grad + RIDGE * old) / diag
    new_ref[...] = new[:, :CLS]
    last = pltpu.make_async_copy(new_ref, new_hbm, out_s.at[N])
    last.start()

    for m in sends:
        m.wait_send()

    @pl.when(r != c)
    def _():
        copy(wown, wown, w1_s.at[0], w1_r.at[0], sib).wait_send()
        copy(us, us, u_s.at[0], u_r.at[0], sib).wait_send()

    for i in range(ND):

        @pl.when(rem(r + i, N) != c)
        def _():
            copy(xb.at[i], xb.at[i], o_s.at[i], o_r.at[0], sib).wait_send()

    def written(i, _):
        pltpu.make_async_copy(gram_ref.at[i], gram_hbm.at[:, rows(i, W)], out_s.at[i]).wait()
        return 0

    lax.fori_loop(0, N, written, 0)
    last.wait()


def shards(embeds, frequencies, phases, labels, weights):
    hbm = pl.BlockSpec(memory_space=pl.ANY)
    buffers = [
        ((ROWS, DIN), BF16),
        ((DIN, W), BF16),
        ((1, W), F32),
        ((1, ROWS), jnp.int32),
        ((W, CLS), F32),
        ((N, W, W), F32),
        ((W, CLS), F32),
        ((N * W, WIDE), BF16),
        (((ND - 1) * W, WIDE), BF16),
        ((N * W, ROWS), BF16),
        ((ND * W, ROWS), BF16),
        ((W, W), F32),
        ((W, W), BF16),
        ((W, N * W), BF16),
        ((W, ROWS), BF16),
        ((N, 16, ROWS), BF16),
        ((W, ROWS), BF16),
        ((N * W, W), F32),
        ((ND, W, W), BF16),
        ((ND - 2, W, W), BF16),
        ((N, W, W), BF16),
        ((W, W), BF16),
        ((W, W), BF16),
    ]
    for dtype in (BF16, BF16, F32, BF16):
        buffers += [((4 * W, n), dtype) for n in GROUPS]
    for _ in range(4):
        buffers += [((2, HALF, n), BF16) for n in GROUPS]
    sem = lambda n: pltpu.SemaphoreType.DMA((n,))
    sems = [sem(7)] * (2 * len(GROUPS)) + [sem(5), sem(N + 1)]
    for n in (2, 2, 4, 4, N, 4, 1, 4, 4, N, N, 1):
        sems += [sem(n), sem(n)]
    sems += [sem(ND), sem(N), sem(ND - 2)]
    return pl.pallas_call(
        kernel,
        out_shape=(
            jax.ShapeDtypeStruct((W, N * W), F32),
            jax.ShapeDtypeStruct((W, CLS), F32),
        ),
        in_specs=[hbm] * 5,
        out_specs=(hbm, hbm),
        scratch_shapes=[pltpu.VMEM(*b) for b in buffers] + sems,
        compiler_params=pltpu.CompilerParams(
            collective_id=0, has_side_effects=True, vmem_limit_bytes=56 * 2**20
        ),
    )(embeds, frequencies, phases.reshape(1, W), labels.reshape(1, ROWS), weights)


def solution(mesh):
    return jax.shard_map(
        shards,
        mesh=mesh,
        in_specs=(
            P("dp", None),
            P(None, ("trow", "tcol")),
            P(("trow", "tcol")),
            P("dp"),
            P(("tcol", "dp"), "trow"),
        ),
        out_specs=(P(("trow", "dp"), "tcol"), P(("tcol", "dp"), "trow")),
        check_vma=False,
    )
```

```python
import jax
import jax.numpy as jnp
from jax import lax
from jax.experimental import pallas as pl
from jax.experimental.pallas import tpu as pltpu
from jax.sharding import PartitionSpec as P

C = 1000
RIDGE = 0.5
STEP_RATE = 0.5
MESH = pl.DeviceIdType.MESH
F32, BF16 = jnp.float32, jnp.bfloat16
NT = (((1,), (1,)), ((), ()))
NN = (((1,), (0,)), ((), ()))

N = 8
W = 128
ROWS = 1024
DIN = 1024
HALF = W // 2
CLS = 125
TOTAL = 8192
ND = 5
GROUPS = (3 * W, 2 * W, W)
INV_PERIOD = 0.15915494309189535
SIN = [
    1.4142135623730951 * q
    for q in (
        6.283185160087748,
        -41.34165503097383,
        81.60100404358543,
        -76.54978157108546,
        39.53670029211564,
    )]


def dot(a, b, dims):
    return lax.dot_general(a, b, dims, preferred_element_type=F32)


def rem(a, b):
    return lax.rem(a, jnp.int32(b))


def place(a):
    return rem(a, 2) * 4 + lax.div(a, jnp.int32(2))


def rows(i, size):
    return pl.ds(pl.multiple_of(i * size, size), size)


def kernel(
    e_hbm, f_hbm, p_hbm, l_hbm, w_hbm, gram_ref, new_ref,
    e_ref, f_ref, p_ref, l_ref, w_ref, pall, prow, pcol,
    fl, fr, feat, featr, wpad, wown, wall, ts, tb, st, ulab, xb, xt, xr, gb, us, ub, *rest
):
    kinds = ("gs", "gr", "gsum", "gb16", "ra", "rb", "cs", "rc", "sem_s", "sem_r")
    groups = [dict(zip(kinds, rest[i :: len(GROUPS)])) for i in range(len(GROUPS))]
    (
        in_s, p_s, p_r, x_s, x_r, q_s, q_r, z_s, z_r, y_s, y_r, sl_s, sl_r, sr_s, sr_r,
        w1_s, w1_r, w2_s, w2_r, w3_s, w3_r, t_s, t_r, a_s, a_r, u_s, u_r, v_s, v_r, o_s, o_r, b_s,
    ) = rest[len(kinds) * len(GROUPS) :]
    r, c, d = lax.axis_index("trow"), lax.axis_index("tcol"), lax.axis_index("dp")
    x, zl = lax.div(c, jnp.int32(2)), rem(c, 2)
    h, k = lax.div(d, jnp.int32(2)), rem(d, 2)
    other = 1 - 2 * zl
    sib = (r, c, 2 * h + 1 - k)
    flipped = (c, r, d)
    zdev = (r, c + other, 2 * rem(h + zl - k + 4, 4) + k)
    zsrc = (r, c + other, 2 * rem(h + zl + k + 3, 4) + k)
    sends = []

    barrier = pltpu.get_barrier_semaphore()

    def here(*dev):
        pl.semaphore_signal(barrier, inc=1, device_id=dev, device_id_type=MESH)

    def greet(i, _):
        here(rem(r + i, N), c, d)
        here(r, rem(c + i, N), d)
        here(r, c, rem(d + i, N))
        return 0

    lax.fori_loop(1, N, greet, 0)
    here(*zsrc)

    @pl.when(r != c)
    def _():
        here(*flipped)

    behind = rem(r - c + N, N)

    turned = jnp.logical_and(behind >= 1, behind <= ND - 2)
    own_relay = jnp.logical_and(turned, c == d)

    @pl.when(turned)
    def _():
        def to_source(i, _):
            @pl.when(jnp.logical_or(c != d, i != d))
            def _():
                here(r, d, i)

            return 0

        lax.fori_loop(0, N, to_source, 0)

    loads = [
        pltpu.make_async_copy(a, b, in_s.at[i])
        for i, (a, b) in enumerate(
            ((f_hbm, f_ref), (p_hbm, p_ref), (w_hbm, w_ref), (l_hbm, l_ref), (e_hbm, e_ref))
        )
    ]
    for m in loads:
        m.start()

    def copy(src, dst, s, t, dev):
        return pltpu.make_async_remote_copy(
            src_ref=src, dst_ref=dst, send_sem=s, recv_sem=t, device_id=dev, device_id_type=MESH
        )

    def send(*args):
        m = copy(*args)
        m.start()
        sends.append(m)

    def arrived(ref, s, t):
        copy(ref, ref, s, t, sib).wait_recv()

    def half(i, core=None):
        return pl.ds(pl.multiple_of(i * W + (k if core is None else core) * HALF, HALF), HALF)

    lane = lax.broadcasted_iota(jnp.int32, (W, W), 1)
    loads[0].wait()
    fl[:W, :] = f_ref[...].astype(F32).T.astype(BF16)
    loads[1].wait()
    pl.semaphore_wait(barrier, 3 * (N - 1) + 1 + ND - 2 + jnp.where(r != c, 1, 0) - jnp.where(own_relay, 1, 0))

    xp, xm, xo = (rem(x + i, 4) * 2 + zl for i in (1, 3, 2))
    slots = [c, xm, xp, xo, c + other, xm + other, xp + other, xo + other]
    ydev = (rem(r + 7, N), c, d)
    own = fl.at[half(0)]

    def quarter(buffer, slot, i):
        return buffer.at[pl.ds(pl.multiple_of(slot * W + k * HALF + i * 32, 32), 32)]

    send(own, fl.at[half(1)], x_s.at[0], x_r.at[0], (r, xp, d))
    send(own, fl.at[half(2)], x_s.at[1], x_r.at[1], (r, xm, d))
    for i in range(2):
        send(quarter(fl, 0, i), quarter(fr, 0, i), y_s.at[i], y_r.at[i], ydev)
    send(own, fl.at[half(4)], z_s.at[0], z_r.at[0], zdev)

    for i in range(1, N):
        send(p_ref, pall.at[c], p_s.at[i], p_r.at[i], (r, rem(c + i, N), d))
    for i in range(1, ND):
        send(p_ref, pall.at[N + i - 1], p_s.at[N + i - 1], p_r.at[N + i - 1], (rem(r + N - i, N), c, d))

    loads[2].wait()
    wpad[...] = jnp.zeros_like(wpad)
    wpad[:, :CLS] = w_ref[...]
    wown[...] = wpad[...].T.astype(BF16)
    wcols = rows(place(d), W)
    wmine = wall.at[:, wcols]

    @pl.when(r != c)
    def _():
        copy(wown, wmine, w1_s.at[0], w1_r.at[0], flipped).start()

    @pl.when(r == c)
    def _():
        wall[:, wcols] = wown[...]

    def cosines(src, phases):
        t = dot(src[...], e_ref[...], NT) * INV_PERIOD + jnp.concatenate(phases, axis=0)
        v = 0.25 - jnp.abs(t - jnp.round(t))
        u = v * v
        w = jnp.full_like(u, SIN[-1])
        for q in SIN[-2::-1]:
            w = w * u + q
        return (w * v).astype(BF16)

    def phases(first, n):
        return [pcol[:, i : i + 1] for i in range(first, first + n)]

    def left(first, n):
        v = cosines(fl.at[first * W : (first + n) * W], phases(first, n) if first else [own_phase])
        for i in range(n):
            feat[rows(place(slots[first + i]), W), :] = v[i * W : (i + 1) * W]

    def right(first, n):
        featr[(first + 1) * W : (first + 1 + n) * W, :] = cosines(
            fr.at[first * W : (first + n) * W], phases(N + first, n)
        )

    def to_sib(i):
        send(fl.at[half(i)], fl.at[half(i)], sl_s.at[i], sl_r.at[i], sib)

    def to_z(i):
        send(fl.at[half(i)], fl.at[half(4 + i)], z_s.at[i], z_r.at[i], zdev)

    def from_z(i):
        arrived(fl.at[half(4 + i)], z_s.at[i], z_r.at[i])
        to_sib(4 + i)

    def from_sib(*which):
        for i in which:
            arrived(fl.at[half(i, 1 - k)], sl_s.at[i], sl_r.at[i])

    def hop_y(i):
        for n in range(2):
            piece = quarter(fr, i, n)
            arrived(piece, y_s.at[2 * i + n], y_r.at[2 * i + n])
            if i < ND - 2:
                m = 2 * i + 2 + n
                send(piece, quarter(fr, i + 1, n), y_s.at[m], y_r.at[m], ydev)
        piece = fr.at[half(i)]
        send(piece, piece, sr_s.at[i], sr_r.at[i], sib)

    def sib_y(*which):
        for i in which:
            arrived(fr.at[half(i, 1 - k)], sr_s.at[i], sr_r.at[i])

    own_phase = (jnp.broadcast_to(p_ref[...], (W, W)) * INV_PERIOD).T[:, 0:1]
    loads[4].wait()
    left(0, 1)
    prow[...] = jnp.zeros_like(prow)
    featr[0:W, :] = feat[rows(place(c), W), :]

    for i, (slot, on) in enumerate(((1, xp), (2, xm))):
        arrived(fl.at[half(slot)], x_s.at[i], x_r.at[i])
        send(quarter(fl, slot, i), quarter(fl, 3, i), q_s.at[i], q_r.at[i], (r, on, d))
        to_z(slot)
        to_sib(slot)
    hop_y(0)
    from_z(0)

    @pl.when(r != c)
    def _():
        arrived(wmine, w1_s.at[0], w1_r.at[0])

    send(wmine, wmine, w3_s.at[0], w3_r.at[0], sib)
    for i in range(1, 4):
        send(wmine, wmine, w2_s.at[i], w2_r.at[i], (r, c, 2 * rem(h + i, 4) + k))

    for i in range(1, N):
        arrived(pall.at[rem(c + N - i, N)], p_s.at[i], p_r.at[i])
    for i in range(N, N + ND - 1):
        arrived(pall.at[i], p_s.at[i], p_r.at[i])
        prow[i : i + 1, :] = pall[i]
    for i in range(1, N):
        prow[i : i + 1, :] = pall[slots[i]]
    pcol[...] = (prow[...] * INV_PERIOD).T
    from_sib(1, 2)
    left(1, 2)
    hop_y(1)
    for i in range(2):
        arrived(quarter(fl, 3, i), q_s.at[i], q_r.at[i])
    to_z(3)
    to_sib(3)
    from_z(1)
    from_z(2)
    for i in range(1, 4):
        piece = wall.at[:, rows(place(2 * rem(h + 4 - i, 4) + k), W)]
        arrived(piece, w2_s.at[i], w2_r.at[i])
        send(piece, piece, w3_s.at[i], w3_r.at[i], sib)
    from_sib(3, 4)
    left(3, 2)
    hop_y(2)
    from_z(3)
    from_sib(5, 6, 7)
    left(5, 3)

    for i in range(4):
        arrived(wall.at[:, rows(place(2 * rem(h + 4 - i, 4) + 1 - k), W)], w3_s.at[i], w3_r.at[i])
    ts[...] = dot(wall[...], feat[...], NN).astype(BF16)
    for i in range(1, N):
        to = rem(r + i, N)
        send(ts.at[rows(to, 16)], tb.at[i], t_s.at[i], t_r.at[i], (to, c, d))

    scale = 1.0 / TOTAL

    def gram_partial(g, first, n):
        cols = featr[first * W : (first + n) * W, :]
        g["gs"][...] = (dot(feat[rows(1 - k, 512), :], cols, NT) * scale).astype(BF16)
        swap(g)
        g["gsum"][...] = dot(feat[rows(k, 512), :], cols, NT) * scale

    def swap(g):
        send(g["gs"], g["gr"], g["sem_s"].at[0], g["sem_r"].at[0], sib)

    hp, hm, ho = rem(h + 1, 4), rem(h + 3, 4), rem(h + 2, 4)
    up, down = (r, c, 2 * hp + k), (r, c, 2 * hm + k)

    def step_one(g):
        arrived(g["gr"], g["sem_s"].at[0], g["sem_r"].at[0])
        g["gsum"][...] = g["gsum"][...] + g["gr"][...].astype(F32)
        g["gb16"][...] = g["gsum"][...].astype(BF16)
        for n, (name, i, at, core, dev) in enumerate(
            (
                ("ra", 0, ho, 0, up),
                ("ra", 1, ho, 1, down),
                ("rb", 0, hp, 1, up),
                ("rb", 1, hm, 0, down),
            )
        ):
            send(g["gb16"].at[half(at, core)], g[name].at[i], g["sem_s"].at[1 + n], g["sem_r"].at[1 + n], dev)

    def step_two(g):
        for i, (at, dev) in enumerate(((hp, up), (hm, down))):
            arrived(g["ra"].at[i], g["sem_s"].at[1 + i], g["sem_r"].at[1 + i])
            g["cs"][i] = (g["gsum"][half(at, i), :] + g["ra"][i].astype(F32)).astype(BF16)
            send(g["cs"].at[i], g["rc"].at[i], g["sem_s"].at[5 + i], g["sem_r"].at[5 + i], dev)

    def step_three(g):
        for i in range(2):
            arrived(g["rb"].at[i], g["sem_s"].at[3 + i], g["sem_r"].at[3 + i])
            arrived(g["rc"].at[i], g["sem_s"].at[5 + i], g["sem_r"].at[5 + i])
        upper = g["gsum"][half(h, 0), :] + g["rc"][0].astype(F32) + g["rb"][1].astype(F32)
        lower = g["gsum"][half(h, 1), :] + g["rb"][0].astype(F32) + g["rc"][1].astype(F32)
        return jnp.concatenate([upper, lower], axis=0)

    def hand_out(g, first, n):
        total = step_three(g)
        for i in range(first, first + n):
            block = total[:, (i - first) * W : (i - first + 1) * W]
            xb[i] = block.astype(BF16)
            to = rem(r + i, N)

            @pl.when(to != c)
            def _():
                copy(xb.at[i], gb.at[c], o_s.at[i], o_r.at[c], (r, to, d)).start()

            @pl.when(to == c)
            def _():
                gb[c] = xb[i]

            if 0 < i < ND - 1:
                xt[i - 1] = block.T.astype(BF16)
                send(xt.at[i - 1], xr.at[i - 1], v_s.at[i - 1], v_r.at[i - 1], (to, c, d))

    def relay(i):
        arrived(xr.at[i - 1], v_s.at[i - 1], v_r.at[i - 1])
        to = rem(r + N - i, N)
        stays = jnp.logical_and(to == c, d == c)

        @pl.when(jnp.logical_not(stays))
        def _():
            copy(xr.at[i - 1], gb.at[d], b_s.at[i - 1], o_r.at[d], (r, to, c)).start()

        @pl.when(stays)
        def _():
            gb[d] = xr[i - 1]

    sib_y(0, 1)
    right(0, 2)
    gram_partial(groups[0], 0, 3)
    hop_y(3)
    step_one(groups[0])

    total = ts[rows(r, 16), :].astype(F32)
    for i in range(1, N):
        arrived(tb.at[i], t_s.at[i], t_r.at[i])
        total = total + tb[i].astype(F32)
    strip = st.at[rows(r, 16)]
    st[rows(r, 16), :] = total.astype(BF16)
    for i in range(1, N):
        send(strip, strip, a_s.at[i], a_r.at[i], (rem(r + i, N), c, d))

    sib_y(2, 3)
    right(2, 2)
    step_two(groups[0])
    gram_partial(groups[1], 3, 2)
    step_one(groups[1])

    loads[3].wait()
    cls = lax.broadcasted_iota(jnp.int32, (W, ROWS), 0)
    onehot = jnp.where(l_ref[...] == cls + c * CLS, 1.0, 0.0).astype(BF16)
    own_f = feat[...].astype(F32)
    diag = jnp.sum(own_f * own_f, axis=1, keepdims=True)
    lane_u = lax.broadcasted_iota(jnp.int32, (N * W, W), 1)
    ulab[...] = jnp.where(lane_u == CLS, diag, -C * dot(feat[...], onehot, NT)) * scale
    hand_out(groups[0], 0, 3)
    step_two(groups[1])

    for i in range(1, N):
        arrived(st.at[rows(rem(r + N - i, N), 16)], a_s.at[i], a_r.at[i])
    ulab[...] = jnp.where(lane_u == CLS, 0.0, dot(feat[...], st[...], NT) * scale) + ulab[...]
    g = groups[2]
    g["gs"][...] = ulab[rows(1 - k, 512), :].astype(BF16)
    swap(g)
    g["gsum"][...] = ulab[rows(k, 512), :]
    step_one(g)
    hand_out(groups[1], 3, 2)
    step_two(g)
    relay(1)
    relay(2)

    delta = rem(c - r + N, N)
    eye = lax.broadcasted_iota(jnp.int32, (W, W), 0) == lane

    total = step_three(g)
    first = total.astype(BF16).astype(F32)
    second = (total - first)[:, CLS : CLS + 1]
    us[...] = jnp.where(lane == CLS + 1, second, total).astype(BF16)

    @pl.when(r != c)
    def _():
        copy(us, ub, u_s.at[0], u_r.at[0], flipped).start()

    @pl.when(r == c)
    def _():
        ub[...] = us[...]

    relay(3)
    for i in range(N):

        @pl.when(jnp.where(delta < ND, i != c, jnp.logical_or(c != d, i != d)))
        def _():
            arrived(gb.at[i], o_s.at[0], o_r.at[i])

        ridge = jnp.where(jnp.logical_and(eye, jnp.logical_and(r == c, d == i)), RIDGE, 0.0)
        gram_ref[:, i * W : (i + 1) * W] = gb[i].astype(F32) + ridge

    @pl.when(r != c)
    def _():
        arrived(ub, u_s.at[0], u_r.at[0])

    grad = ub[...].astype(F32)
    old = wpad[...]
    diag = grad[:, CLS : CLS + 1] + grad[:, CLS + 1 : CLS + 2] + RIDGE
    new = old - STEP_RATE * (grad + RIDGE * old) / diag
    new_ref[...] = new[:, :CLS]

    for m in sends:
        m.wait_send()

    @pl.when(r != c)
    def _():
        copy(wown, wown, w1_s.at[0], w1_r.at[0], sib).wait_send()
        copy(us, us, u_s.at[0], u_r.at[0], sib).wait_send()

    for i in range(ND):

        @pl.when(rem(r + i, N) != c)
        def _():
            copy(xb.at[i], xb.at[i], o_s.at[i], o_r.at[0], sib).wait_send()

    for i in range(1, ND - 1):

        @pl.when(jnp.logical_not(jnp.logical_and(rem(r + N - i, N) == c, d == c)))
        def _():
            copy(xr.at[0], xr.at[0], b_s.at[i - 1], o_r.at[0], sib).wait_send()


def shards(embeds, frequencies, phases, labels, weights):
    hbm = pl.BlockSpec(memory_space=pl.ANY)
    vmem = pl.BlockSpec(memory_space=pltpu.VMEM)
    buffers = [
        ((ROWS, DIN), BF16),
        ((DIN, W), BF16),
        ((1, W), F32),
        ((1, ROWS), jnp.int32),
        ((W, CLS), F32),
        ((N + ND - 1, 1, W), F32),
        ((W, W), F32),
        ((W, W), F32),
        ((N * W, DIN), BF16),
        (((ND - 1) * W, DIN), BF16),
        ((N * W, ROWS), BF16),
        ((ND * W, ROWS), BF16),
        ((W, W), F32),
        ((W, W), BF16),
        ((W, N * W), BF16),
        ((W, ROWS), BF16),
        ((N, 16, ROWS), BF16),
        ((W, ROWS), BF16),
        ((N * W, W), F32),
        ((ND, W, W), BF16),
        ((ND - 2, W, W), BF16),
        ((ND - 2, W, W), BF16),
        ((N, W, W), BF16),
        ((W, W), BF16),
        ((W, W), BF16),
    ]
    for dtype in (BF16, BF16, F32, BF16):
        buffers += [((4 * W, n), dtype) for n in GROUPS]
    for _ in range(4):
        buffers += [((2, HALF, n), BF16) for n in GROUPS]
    sem = lambda n: pltpu.SemaphoreType.DMA((n,))
    sems = [sem(7)] * (2 * len(GROUPS)) + [sem(5), sem(N + ND - 1), sem(N + ND - 1)]
    for n in (2, 2, 4, 2 * ND - 2, N, 4, 1, 4, 4, N, N, 1, ND - 2):
        sems += [sem(n), sem(n)]
    sems += [sem(ND), sem(N), sem(ND - 2)]
    return pl.pallas_call(
        kernel,
        out_shape=(
            jax.ShapeDtypeStruct((W, N * W), F32),
            jax.ShapeDtypeStruct((W, CLS), F32),
        ),
        in_specs=[hbm] * 5,
        out_specs=(vmem, vmem),
        scratch_shapes=[pltpu.VMEM(*b) for b in buffers] + sems,
        compiler_params=pltpu.CompilerParams(
            collective_id=0, has_side_effects=True, vmem_limit_bytes=56 * 2**20
        ),
    )(embeds, frequencies, phases.reshape(1, W), labels.reshape(1, ROWS), weights)


def solution(mesh):
    return jax.shard_map(
        shards,
        mesh=mesh,
        in_specs=(
            P("dp", None),
            P(None, ("trow", "tcol")),
            P(("trow", "tcol")),
            P("dp"),
            P(("tcol", "dp"), "trow"),
        ),
        out_specs=(P(("trow", "dp"), "tcol"), P(("tcol", "dp"), "trow")),
        check_vma=False,
    )
```

```python
import jax
import jax.numpy as jnp
from jax import lax
from jax.experimental import pallas as pl
from jax.experimental.pallas import tpu as pltpu
from jax.sharding import PartitionSpec as P

C = 1000
RIDGE = 0.5
STEP_RATE = 0.5
MESH = pl.DeviceIdType.MESH
F32, BF16 = jnp.float32, jnp.bfloat16
NT = (((1,), (1,)), ((), ()))
NN = (((1,), (0,)), ((), ()))

N = 8
W = 128
ROWS = 1024
DIN = 1024
HALF = W // 2
CLS = 125
TOTAL = 8192
ND = 5
GROUPS = (3 * W, 2 * W, W)
INV_PERIOD = 0.15915494309189535
SIN = [
    1.4142135623730951 * q
    for q in (
        6.283185160087748,
        -41.34165503097383,
        81.60100404358543,
        -76.54978157108546,
        39.53670029211564,
    )]


def dot(a, b, dims):
    return lax.dot_general(a, b, dims, preferred_element_type=F32)


def rem(a, b):
    return lax.rem(a, jnp.int32(b))


def place(a):
    return rem(a, 2) * 4 + lax.div(a, jnp.int32(2))


def rows(i, size):
    return pl.ds(pl.multiple_of(i * size, size), size)


def kernel(
    e_hbm, f_hbm, p_hbm, l_hbm, w_hbm, gram_ref, new_ref,
    e_ref, f_ref, p_ref, l_ref, w_ref, pall, prow, pcol,
    fl, fr, feat, featr, wpad, wown, wall, ts, tb, st, ulab, xb, xt, xr, gb, us, ub, uq, *rest
):
    kinds = ("gs", "gr", "gsum", "gb16", "ra", "rb", "cs", "rc", "sem_s", "sem_r")
    groups = [dict(zip(kinds, rest[i :: len(GROUPS)])) for i in range(len(GROUPS))]
    (
        in_s, p_s, p_r, x_s, x_r, q_s, q_r, z_s, z_r, y_s, y_r, sl_s, sl_r, sr_s, sr_r,
        w1_s, w1_r, w2_s, w2_r, w3_s, w3_r, t_s, t_r, a_s, a_r, u_s, u_r, v_s, v_r, o_s, o_r, b_s,
    ) = rest[len(kinds) * len(GROUPS) :]
    r, c, d = lax.axis_index("trow"), lax.axis_index("tcol"), lax.axis_index("dp")
    x, zl = lax.div(c, jnp.int32(2)), rem(c, 2)
    h, k = lax.div(d, jnp.int32(2)), rem(d, 2)
    other = 1 - 2 * zl
    sib = (r, c, 2 * h + 1 - k)
    flipped = (c, r, d)
    zdev = (r, c + other, 2 * rem(h + zl - k + 4, 4) + k)
    zsrc = (r, c + other, 2 * rem(h + zl + k + 3, 4) + k)
    sends = []

    barrier = pltpu.get_barrier_semaphore()

    def here(*dev):
        pl.semaphore_signal(barrier, inc=1, device_id=dev, device_id_type=MESH)

    def greet(i, _):
        here(rem(r + i, N), c, d)
        here(r, rem(c + i, N), d)
        here(r, c, rem(d + i, N))
        return 0

    lax.fori_loop(1, N, greet, 0)
    here(*zsrc)

    @pl.when(r != c)
    def _():
        here(*flipped)

    behind = rem(r - c + N, N)

    turned = jnp.logical_and(behind >= 1, behind <= ND - 2)
    own_relay = jnp.logical_and(turned, c == d)

    @pl.when(turned)
    def _():
        def to_source(i, _):
            @pl.when(jnp.logical_or(c != d, i != d))
            def _():
                here(r, d, i)

            return 0

        lax.fori_loop(0, N, to_source, 0)

    loads = [
        pltpu.make_async_copy(a, b, in_s.at[i])
        for i, (a, b) in enumerate(
            ((f_hbm, f_ref), (p_hbm, p_ref), (w_hbm, w_ref), (l_hbm, l_ref), (e_hbm, e_ref))
        )
    ]
    for m in loads[:3]:
        m.start()

    def copy(src, dst, s, t, dev):
        return pltpu.make_async_remote_copy(
            src_ref=src, dst_ref=dst, send_sem=s, recv_sem=t, device_id=dev, device_id_type=MESH
        )

    def send(*args):
        m = copy(*args)
        m.start()
        sends.append(m)

    def arrived(ref, s, t):
        copy(ref, ref, s, t, sib).wait_recv()

    def half(i, core=None):
        return pl.ds(pl.multiple_of(i * W + (k if core is None else core) * HALF, HALF), HALF)

    lane = lax.broadcasted_iota(jnp.int32, (W, W), 1)
    loads[0].wait()
    for m in loads[3:]:
        m.start()
    fl[:W, :] = f_ref[...].astype(F32).T.astype(BF16)
    loads[1].wait()
    pl.semaphore_wait(barrier, 3 * (N - 1) + 1 + ND - 2 + jnp.where(r != c, 1, 0) - jnp.where(own_relay, 1, 0))

    xp, xm, xo = (rem(x + i, 4) * 2 + zl for i in (1, 3, 2))
    slots = [c, xm, xp, xo, c + other, xm + other, xp + other, xo + other]
    ydev = (rem(r + 7, N), c, d)
    own = fl.at[half(0)]

    def quarter(buffer, slot, i):
        return buffer.at[pl.ds(pl.multiple_of(slot * W + k * HALF + i * 32, 32), 32)]

    send(own, fl.at[half(1)], x_s.at[0], x_r.at[0], (r, xp, d))
    send(own, fl.at[half(2)], x_s.at[1], x_r.at[1], (r, xm, d))
    send(own, fr.at[half(0)], y_s.at[0], y_r.at[0], ydev)
    send(own, fl.at[half(4)], z_s.at[0], z_r.at[0], zdev)

    for i in range(1, N):
        send(p_ref, pall.at[c], p_s.at[i], p_r.at[i], (r, rem(c + i, N), d))
    for i in range(1, ND):
        send(p_ref, pall.at[N + i - 1], p_s.at[N + i - 1], p_r.at[N + i - 1], (rem(r + N - i, N), c, d))

    loads[2].wait()
    wpad[...] = jnp.zeros_like(wpad)
    wpad[:, :CLS] = w_ref[...]
    wown[...] = wpad[...].T.astype(BF16)
    wcols = rows(place(d), W)
    wmine = wall.at[:, wcols]

    @pl.when(r != c)
    def _():
        copy(wown, wmine, w1_s.at[0], w1_r.at[0], flipped).start()

    @pl.when(r == c)
    def _():
        wall[:, wcols] = wown[...]

    def cosines(src, phases):
        t = dot(src[...], e_ref[...], NT) * INV_PERIOD + jnp.concatenate(phases, axis=0)
        v = 0.25 - jnp.abs(t - jnp.round(t))
        u = v * v
        w = jnp.full_like(u, SIN[-1])
        for q in SIN[-2::-1]:
            w = w * u + q
        return (w * v).astype(BF16)

    def phases(first, n):
        return [pcol[:, i : i + 1] for i in range(first, first + n)]

    def left(first, n):
        v = cosines(fl.at[first * W : (first + n) * W], phases(first, n) if first else [own_phase])
        for i in range(n):
            feat[rows(place(slots[first + i]), W), :] = v[i * W : (i + 1) * W]

    def right(first, n):
        featr[(first + 1) * W : (first + 1 + n) * W, :] = cosines(
            fr.at[first * W : (first + n) * W], phases(N + first, n)
        )

    def to_sib(i):
        send(fl.at[half(i)], fl.at[half(i)], sl_s.at[i], sl_r.at[i], sib)

    def to_z(i):
        send(fl.at[half(i)], fl.at[half(4 + i)], z_s.at[i], z_r.at[i], zdev)

    def from_z(i):
        arrived(fl.at[half(4 + i)], z_s.at[i], z_r.at[i])
        to_sib(4 + i)

    def from_sib(*which):
        for i in which:
            arrived(fl.at[half(i, 1 - k)], sl_s.at[i], sl_r.at[i])

    def hop_y(i):
        piece = fr.at[half(i)]
        arrived(piece, y_s.at[i], y_r.at[i])
        if i < ND - 2:
            send(piece, fr.at[half(i + 1)], y_s.at[i + 1], y_r.at[i + 1], ydev)
        send(piece, piece, sr_s.at[i], sr_r.at[i], sib)

    def sib_y(*which):
        for i in which:
            arrived(fr.at[half(i, 1 - k)], sr_s.at[i], sr_r.at[i])

    own_phase = (jnp.broadcast_to(p_ref[...], (W, W)) * INV_PERIOD).T[:, 0:1]
    loads[4].wait()
    left(0, 1)
    prow[...] = jnp.zeros_like(prow)
    featr[0:W, :] = feat[rows(place(c), W), :]

    for i, (slot, on) in enumerate(((1, xp), (2, xm))):
        arrived(fl.at[half(slot)], x_s.at[i], x_r.at[i])
        send(quarter(fl, slot, i), quarter(fl, 3, i), q_s.at[i], q_r.at[i], (r, on, d))
        to_z(slot)
        to_sib(slot)
    hop_y(0)
    from_z(0)

    for i in range(1, N):
        arrived(pall.at[rem(c + N - i, N)], p_s.at[i], p_r.at[i])
    for i in range(N, N + ND - 1):
        arrived(pall.at[i], p_s.at[i], p_r.at[i])
        prow[i : i + 1, :] = pall[i]
    for i in range(1, N):
        prow[i : i + 1, :] = pall[slots[i]]
    pcol[...] = (prow[...] * INV_PERIOD).T
    from_sib(1, 2)
    left(1, 2)
    hop_y(1)
    for i in range(2):
        arrived(quarter(fl, 3, i), q_s.at[i], q_r.at[i])
    to_z(3)
    to_sib(3)
    @pl.when(r != c)
    def _():
        arrived(wmine, w1_s.at[0], w1_r.at[0])

    send(wmine, wmine, w3_s.at[0], w3_r.at[0], sib)
    for i in range(1, 4):
        send(wmine, wmine, w2_s.at[i], w2_r.at[i], (r, c, 2 * rem(h + i, 4) + k))

    from_z(1)
    from_z(2)
    from_sib(3, 4)
    left(3, 2)
    from_sib(5, 6)
    left(5, 2)
    for i in range(1, 4):
        piece = wall.at[:, rows(place(2 * rem(h + 4 - i, 4) + k), W)]
        arrived(piece, w2_s.at[i], w2_r.at[i])
        send(piece, piece, w3_s.at[i], w3_r.at[i], sib)
    from_z(3)
    hop_y(2)
    from_sib(7)
    left(7, 1)

    for i in range(4):
        arrived(wall.at[:, rows(place(2 * rem(h + 4 - i, 4) + 1 - k), W)], w3_s.at[i], w3_r.at[i])
    ts[...] = dot(wall[...], feat[...], NN).astype(BF16)
    for i in range(1, N):
        to = rem(r + i, N)
        send(ts.at[rows(to, 16)], tb.at[i], t_s.at[i], t_r.at[i], (to, c, d))

    scale = 1.0 / TOTAL

    def gram_partial(g, first, n):
        cols = featr[first * W : (first + n) * W, :]
        g["gs"][...] = (dot(feat[rows(1 - k, 512), :], cols, NT) * scale).astype(BF16)
        swap(g)
        g["gsum"][...] = dot(feat[rows(k, 512), :], cols, NT) * scale

    def swap(g):
        send(g["gs"], g["gr"], g["sem_s"].at[0], g["sem_r"].at[0], sib)

    hp, hm, ho = rem(h + 1, 4), rem(h + 3, 4), rem(h + 2, 4)
    up, down = (r, c, 2 * hp + k), (r, c, 2 * hm + k)

    def step_one(g):
        arrived(g["gr"], g["sem_s"].at[0], g["sem_r"].at[0])
        g["gsum"][...] = g["gsum"][...] + g["gr"][...].astype(F32)
        g["gb16"][...] = g["gsum"][...].astype(BF16)
        for n, (name, i, at, core, dev) in enumerate(
            (
                ("ra", 0, ho, 0, up),
                ("ra", 1, ho, 1, down),
                ("rb", 0, hp, 1, up),
                ("rb", 1, hm, 0, down),
            )
        ):
            send(g["gb16"].at[half(at, core)], g[name].at[i], g["sem_s"].at[1 + n], g["sem_r"].at[1 + n], dev)

    def step_two(g):
        for i, (at, dev) in enumerate(((hp, up), (hm, down))):
            arrived(g["ra"].at[i], g["sem_s"].at[1 + i], g["sem_r"].at[1 + i])
            g["cs"][i] = (g["gsum"][half(at, i), :] + g["ra"][i].astype(F32)).astype(BF16)
            send(g["cs"].at[i], g["rc"].at[i], g["sem_s"].at[5 + i], g["sem_r"].at[5 + i], dev)

    def step_three(g):
        for i in range(2):
            arrived(g["rb"].at[i], g["sem_s"].at[3 + i], g["sem_r"].at[3 + i])
            arrived(g["rc"].at[i], g["sem_s"].at[5 + i], g["sem_r"].at[5 + i])
        upper = g["gsum"][half(h, 0), :] + g["rc"][0].astype(F32) + g["rb"][1].astype(F32)
        lower = g["gsum"][half(h, 1), :] + g["rb"][0].astype(F32) + g["rc"][1].astype(F32)
        return jnp.concatenate([upper, lower], axis=0)

    def hand_out(g, first, n):
        total = step_three(g)
        for i in range(first, first + n):
            block = total[:, (i - first) * W : (i - first + 1) * W]
            xb[i] = block.astype(BF16)
            to = rem(r + i, N)

            @pl.when(to != c)
            def _():
                copy(xb.at[i], gb.at[c], o_s.at[i], o_r.at[c], (r, to, d)).start()

            @pl.when(to == c)
            def _():
                gb[c] = xb[i]

            if 0 < i < ND - 1:
                xt[i - 1] = block.T.astype(BF16)
                send(xt.at[i - 1], xr.at[i - 1], v_s.at[i - 1], v_r.at[i - 1], (to, c, d))

    def relay(i):
        arrived(xr.at[i - 1], v_s.at[i - 1], v_r.at[i - 1])
        to = rem(r + N - i, N)
        stays = jnp.logical_and(to == c, d == c)

        @pl.when(jnp.logical_not(stays))
        def _():
            copy(xr.at[i - 1], gb.at[d], b_s.at[i - 1], o_r.at[d], (r, to, c)).start()

        @pl.when(stays)
        def _():
            gb[d] = xr[i - 1]

    sib_y(0, 1)
    right(0, 2)
    gram_partial(groups[0], 0, 3)
    step_one(groups[0])
    hop_y(3)

    sib_y(2, 3)
    right(2, 2)
    step_two(groups[0])
    total = ts[rows(r, 16), :].astype(F32)
    for i in range(1, N):
        arrived(tb.at[i], t_s.at[i], t_r.at[i])
        total = total + tb[i].astype(F32)
    strip = st.at[rows(r, 16)]
    st[rows(r, 16), :] = total.astype(BF16)
    for i in range(1, N):
        send(strip, strip, a_s.at[i], a_r.at[i], (rem(r + i, N), c, d))

    gram_partial(groups[1], 3, 2)
    step_one(groups[1])

    loads[3].wait()
    cls = lax.broadcasted_iota(jnp.int32, (W, ROWS), 0)
    onehot = jnp.where(l_ref[...] == cls + c * CLS, 1.0, 0.0).astype(BF16)
    own_f = feat[...].astype(F32)
    diag = jnp.sum(own_f * own_f, axis=1, keepdims=True)
    lane_u = lax.broadcasted_iota(jnp.int32, (N * W, W), 1)
    ulab[...] = jnp.where(lane_u == CLS, diag, -C * dot(feat[...], onehot, NT)) * scale
    step_two(groups[1])
    hand_out(groups[0], 0, 3)

    for i in range(1, N):
        arrived(st.at[rows(rem(r + N - i, N), 16)], a_s.at[i], a_r.at[i])
    ulab[...] = jnp.where(lane_u == CLS, 0.0, dot(feat[...], st[...], NT) * scale) + ulab[...]
    g = groups[2]
    g["gs"][...] = ulab[rows(1 - k, 512), :].astype(BF16)
    swap(g)
    g["gsum"][...] = ulab[rows(k, 512), :]
    arrived(g["gr"], g["sem_s"].at[0], g["sem_r"].at[0])
    g["gsum"][...] = g["gsum"][...] + g["gr"][...].astype(F32)
    g["gb16"][...] = g["gsum"][...].astype(BF16)
    for i in range(1, 4):
        to = rem(h + i, 4)
        send(g["gb16"].at[rows(to, W)], uq.at[i - 1], g["sem_s"].at[i], g["sem_r"].at[i], (r, c, 2 * to + k))
    hand_out(groups[1], 3, 2)
    relay(1)
    relay(2)

    delta = rem(c - r + N, N)
    eye = lax.broadcasted_iota(jnp.int32, (W, W), 0) == lane

    total = g["gsum"][rows(h, W), :]
    for i in range(1, 4):
        arrived(uq.at[i - 1], g["sem_s"].at[i], g["sem_r"].at[i])
        total = total + uq[i - 1].astype(F32)
    first = total.astype(BF16).astype(F32)
    second = (total - first)[:, CLS : CLS + 1]
    us[...] = jnp.where(lane == CLS + 1, second, total).astype(BF16)

    @pl.when(r != c)
    def _():
        copy(us, ub, u_s.at[0], u_r.at[0], flipped).start()

    @pl.when(r == c)
    def _():
        ub[...] = us[...]

    relay(3)
    for i in range(N):

        @pl.when(jnp.where(delta < ND, i != c, jnp.logical_or(c != d, i != d)))
        def _():
            arrived(gb.at[i], o_s.at[0], o_r.at[i])

        ridge = jnp.where(jnp.logical_and(eye, jnp.logical_and(r == c, d == i)), RIDGE, 0.0)
        gram_ref[:, i * W : (i + 1) * W] = gb[i].astype(F32) + ridge

    @pl.when(r != c)
    def _():
        arrived(ub, u_s.at[0], u_r.at[0])

    grad = ub[...].astype(F32)
    old = wpad[...]
    diag = grad[:, CLS : CLS + 1] + grad[:, CLS + 1 : CLS + 2] + RIDGE
    new = old - STEP_RATE * (grad + RIDGE * old) / diag
    new_ref[...] = new[:, :CLS]

    for m in sends:
        m.wait_send()

    @pl.when(r != c)
    def _():
        copy(wown, wown, w1_s.at[0], w1_r.at[0], sib).wait_send()
        copy(us, us, u_s.at[0], u_r.at[0], sib).wait_send()

    for i in range(ND):

        @pl.when(rem(r + i, N) != c)
        def _():
            copy(xb.at[i], xb.at[i], o_s.at[i], o_r.at[0], sib).wait_send()

    for i in range(1, ND - 1):

        @pl.when(jnp.logical_not(jnp.logical_and(rem(r + N - i, N) == c, d == c)))
        def _():
            copy(xr.at[0], xr.at[0], b_s.at[i - 1], o_r.at[0], sib).wait_send()


def shards(embeds, frequencies, phases, labels, weights):
    hbm = pl.BlockSpec(memory_space=pl.ANY)
    vmem = pl.BlockSpec(memory_space=pltpu.VMEM)
    buffers = [
        ((ROWS, DIN), BF16),
        ((DIN, W), BF16),
        ((1, W), F32),
        ((1, ROWS), jnp.int32),
        ((W, CLS), F32),
        ((N + ND - 1, 1, W), F32),
        ((W, W), F32),
        ((W, W), F32),
        ((N * W, DIN), BF16),
        (((ND - 1) * W, DIN), BF16),
        ((N * W, ROWS), BF16),
        ((ND * W, ROWS), BF16),
        ((W, W), F32),
        ((W, W), BF16),
        ((W, N * W), BF16),
        ((W, ROWS), BF16),
        ((N, 16, ROWS), BF16),
        ((W, ROWS), BF16),
        ((N * W, W), F32),
        ((ND, W, W), BF16),
        ((ND - 2, W, W), BF16),
        ((ND - 2, W, W), BF16),
        ((N, W, W), BF16),
        ((W, W), BF16),
        ((W, W), BF16),
        ((3, W, W), BF16),
    ]
    for dtype in (BF16, BF16, F32, BF16):
        buffers += [((4 * W, n), dtype) for n in GROUPS]
    for _ in range(4):
        buffers += [((2, HALF, n), BF16) for n in GROUPS]
    sem = lambda n: pltpu.SemaphoreType.DMA((n,))
    sems = [sem(7)] * (2 * len(GROUPS)) + [sem(5), sem(N + ND - 1), sem(N + ND - 1)]
    for n in (2, 2, 4, ND - 1, N, 4, 1, 4, 4, N, N, 1, ND - 2):
        sems += [sem(n), sem(n)]
    sems += [sem(ND), sem(N), sem(ND - 2)]
    return pl.pallas_call(
        kernel,
        out_shape=(
            jax.ShapeDtypeStruct((W, N * W), F32),
            jax.ShapeDtypeStruct((W, CLS), F32),
        ),
        in_specs=[hbm] * 5,
        out_specs=(vmem, vmem),
        scratch_shapes=[pltpu.VMEM(*b) for b in buffers] + sems,
        compiler_params=pltpu.CompilerParams(
            collective_id=0, has_side_effects=True, vmem_limit_bytes=56 * 2**20
        ),
    )(embeds, frequencies, phases.reshape(1, W), labels.reshape(1, ROWS), weights)


def solution(mesh):
    return jax.shard_map(
        shards,
        mesh=mesh,
        in_specs=(
            P("dp", None),
            P(None, ("trow", "tcol")),
            P(("trow", "tcol")),
            P("dp"),
            P(("tcol", "dp"), "trow"),
        ),
        out_specs=(P(("trow", "dp"), "tcol"), P(("tcol", "dp"), "trow")),
        check_vma=False,
    )
```

```python
import jax
import jax.numpy as jnp
from jax import lax
from jax.experimental import pallas as pl
from jax.experimental.pallas import tpu as pltpu
from jax.sharding import PartitionSpec as P

C = 1000
RIDGE = 0.5
STEP_RATE = 0.5
MESH = pl.DeviceIdType.MESH
F32, BF16 = jnp.float32, jnp.bfloat16
NT = (((1,), (1,)), ((), ()))
NN = (((1,), (0,)), ((), ()))

N = 8
W = 128
ROWS = 1024
DIN = 1024
HALF = W // 2
CLS = 125
TOTAL = 8192
ND = 5
GROUPS = (3 * W, 2 * W, W)
INV_PERIOD = 0.15915494309189535
SIN = [
    1.4142135623730951 * q
    for q in (
        6.283185160087748,
        -41.34165503097383,
        81.60100404358543,
        -76.54978157108546,
        39.53670029211564,
    )]


def dot(a, b, dims):
    return lax.dot_general(a, b, dims, preferred_element_type=F32)


def rem(a, b):
    return lax.rem(a, jnp.int32(b))


def place(a):
    return rem(a, 2) * 4 + lax.div(a, jnp.int32(2))


def rows(i, size):
    return pl.ds(pl.multiple_of(i * size, size), size)


def kernel(
    e_hbm, f_hbm, p_hbm, l_hbm, w_hbm, gram_ref, new_ref,
    e_ref, f_ref, p_ref, l_ref, w_ref, pall, prow, pcol,
    fl, fr, feat, featr, wpad, wown, wall, ts, tb, st, ulab, xb, xt, xr, gb, us, ub, uq, *rest
):
    kinds = ("gs", "gr", "gsum", "gb16", "ra", "rb", "cs", "rc", "sem_s", "sem_r")
    groups = [dict(zip(kinds, rest[i :: len(GROUPS)])) for i in range(len(GROUPS))]
    (
        in_s, p_s, p_r, x_s, x_r, q_s, q_r, z_s, z_r, y_s, y_r, sl_s, sl_r, sr_s, sr_r,
        w1_s, w1_r, w2_s, w2_r, w3_s, w3_r, t_s, t_r, a_s, a_r, u_s, u_r, v_s, v_r, o_s, o_r, b_s,
    ) = rest[len(kinds) * len(GROUPS) :]
    r, c, d = lax.axis_index("trow"), lax.axis_index("tcol"), lax.axis_index("dp")
    x, zl = lax.div(c, jnp.int32(2)), rem(c, 2)
    h, k = lax.div(d, jnp.int32(2)), rem(d, 2)
    other = 1 - 2 * zl
    sib = (r, c, 2 * h + 1 - k)
    flipped = (c, r, d)
    zdev = (r, c + other, 2 * rem(h + zl - k + 4, 4) + k)
    zsrc = (r, c + other, 2 * rem(h + zl + k + 3, 4) + k)
    sends = []

    barrier = pltpu.get_barrier_semaphore()

    def here(*dev):
        pl.semaphore_signal(barrier, inc=1, device_id=dev, device_id_type=MESH)

    def greet(i, _):
        here(rem(r + i, N), c, d)
        here(r, rem(c + i, N), d)
        here(r, c, rem(d + i, N))
        return 0

    lax.fori_loop(1, N, greet, 0)
    here(*zsrc)

    @pl.when(r != c)
    def _():
        here(*flipped)

    behind = rem(r - c + N, N)

    turned = jnp.logical_and(behind >= 1, behind <= ND - 2)
    own_relay = jnp.logical_and(turned, c == d)

    @pl.when(turned)
    def _():
        def to_source(i, _):
            @pl.when(jnp.logical_or(c != d, i != d))
            def _():
                here(r, d, i)

            return 0

        lax.fori_loop(0, N, to_source, 0)

    loads = [
        pltpu.make_async_copy(a, b, in_s.at[i])
        for i, (a, b) in enumerate(
            ((f_hbm, f_ref), (p_hbm, p_ref), (w_hbm, w_ref), (l_hbm, l_ref), (e_hbm, e_ref))
        )
    ]
    for m in loads[:3]:
        m.start()

    def copy(src, dst, s, t, dev):
        return pltpu.make_async_remote_copy(
            src_ref=src, dst_ref=dst, send_sem=s, recv_sem=t, device_id=dev, device_id_type=MESH
        )

    def send(*args):
        m = copy(*args)
        m.start()
        sends.append(m)

    def arrived(ref, s, t):
        copy(ref, ref, s, t, sib).wait_recv()

    def half(i, core=None):
        return pl.ds(pl.multiple_of(i * W + (k if core is None else core) * HALF, HALF), HALF)

    lane = lax.broadcasted_iota(jnp.int32, (W, W), 1)
    loads[0].wait()
    for m in loads[3:]:
        m.start()
    fl[:W, :] = f_ref[...].astype(F32).T.astype(BF16)
    loads[1].wait()
    pl.semaphore_wait(barrier, 3 * (N - 1) + 1 + ND - 2 + jnp.where(r != c, 1, 0) - jnp.where(own_relay, 1, 0))

    xp, xm, xo = (rem(x + i, 4) * 2 + zl for i in (1, 3, 2))
    slots = [c, xm, xp, xo, c + other, xm + other, xp + other, xo + other]
    ydev = (rem(r + 7, N), c, d)
    own = fl.at[half(0)]

    def quarter(buffer, slot, i):
        return buffer.at[pl.ds(pl.multiple_of(slot * W + k * HALF + i * 32, 32), 32)]

    send(own, fr.at[half(0)], y_s.at[0], y_r.at[0], ydev)
    send(own, fl.at[half(1)], x_s.at[0], x_r.at[0], (r, xp, d))
    send(own, fl.at[half(2)], x_s.at[1], x_r.at[1], (r, xm, d))
    send(own, fl.at[half(4)], z_s.at[0], z_r.at[0], zdev)

    for i in range(1, N):
        send(p_ref, pall.at[c], p_s.at[i], p_r.at[i], (r, rem(c + i, N), d))
    for i in range(1, ND):
        send(p_ref, pall.at[N + i - 1], p_s.at[N + i - 1], p_r.at[N + i - 1], (rem(r + N - i, N), c, d))

    loads[2].wait()
    wpad[...] = jnp.zeros_like(wpad)
    wpad[:, :CLS] = w_ref[...]
    wown[...] = wpad[...].T.astype(BF16)
    wcols = rows(place(d), W)
    wmine = wall.at[:, wcols]

    @pl.when(r != c)
    def _():
        copy(wown, wmine, w1_s.at[0], w1_r.at[0], flipped).start()

    @pl.when(r == c)
    def _():
        wall[:, wcols] = wown[...]

    def cosines(src, phases):
        t = dot(src[...], e_ref[...], NT) * INV_PERIOD + jnp.concatenate(phases, axis=0)
        v = 0.25 - jnp.abs(t - jnp.round(t))
        u = v * v
        w = jnp.full_like(u, SIN[-1])
        for q in SIN[-2::-1]:
            w = w * u + q
        return (w * v).astype(BF16)

    def phases(first, n):
        return [pcol[:, i : i + 1] for i in range(first, first + n)]

    def left(first, n):
        v = cosines(fl.at[first * W : (first + n) * W], phases(first, n) if first else [own_phase])
        for i in range(n):
            feat[rows(place(slots[first + i]), W), :] = v[i * W : (i + 1) * W]

    def right(first, n):
        featr[(first + 1) * W : (first + 1 + n) * W, :] = cosines(
            fr.at[first * W : (first + n) * W], phases(N + first, n)
        )

    def to_sib(i):
        send(fl.at[half(i)], fl.at[half(i)], sl_s.at[i], sl_r.at[i], sib)

    def to_z(i):
        send(fl.at[half(i)], fl.at[half(4 + i)], z_s.at[i], z_r.at[i], zdev)

    def from_z(i):
        arrived(fl.at[half(4 + i)], z_s.at[i], z_r.at[i])
        to_sib(4 + i)

    def from_sib(*which):
        for i in which:
            arrived(fl.at[half(i, 1 - k)], sl_s.at[i], sl_r.at[i])

    def hop_y(i):
        piece = fr.at[half(i)]
        arrived(piece, y_s.at[i], y_r.at[i])
        if i < ND - 2:
            send(piece, fr.at[half(i + 1)], y_s.at[i + 1], y_r.at[i + 1], ydev)
        send(piece, piece, sr_s.at[i], sr_r.at[i], sib)

    def sib_y(*which):
        for i in which:
            arrived(fr.at[half(i, 1 - k)], sr_s.at[i], sr_r.at[i])

    own_phase = (jnp.broadcast_to(p_ref[...], (W, W)) * INV_PERIOD).T[:, 0:1]
    loads[4].wait()
    left(0, 1)
    prow[...] = jnp.zeros_like(prow)
    featr[0:W, :] = feat[rows(place(c), W), :]

    hop_y(0)
    for i, (slot, on) in enumerate(((1, xp), (2, xm))):
        arrived(fl.at[half(slot)], x_s.at[i], x_r.at[i])
        send(quarter(fl, slot, i), quarter(fl, 3, i), q_s.at[i], q_r.at[i], (r, on, d))
        to_z(slot)
        to_sib(slot)
    from_z(0)

    for i in range(1, N):
        arrived(pall.at[rem(c + N - i, N)], p_s.at[i], p_r.at[i])
    for i in range(N, N + ND - 1):
        arrived(pall.at[i], p_s.at[i], p_r.at[i])
        prow[i : i + 1, :] = pall[i]
    for i in range(1, N):
        prow[i : i + 1, :] = pall[slots[i]]
    pcol[...] = (prow[...] * INV_PERIOD).T
    from_sib(1, 2)
    left(1, 2)
    hop_y(1)
    for i in range(2):
        arrived(quarter(fl, 3, i), q_s.at[i], q_r.at[i])
    to_z(3)
    to_sib(3)
    @pl.when(r != c)
    def _():
        arrived(wmine, w1_s.at[0], w1_r.at[0])

    send(wmine, wmine, w3_s.at[0], w3_r.at[0], sib)
    for i in range(1, 4):
        send(wmine, wmine, w2_s.at[i], w2_r.at[i], (r, c, 2 * rem(h + i, 4) + k))

    from_z(1)
    from_z(2)
    from_sib(3, 4)
    left(3, 2)
    from_sib(5, 6)
    left(5, 2)
    for i in range(1, 4):
        piece = wall.at[:, rows(place(2 * rem(h + 4 - i, 4) + k), W)]
        arrived(piece, w2_s.at[i], w2_r.at[i])
        send(piece, piece, w3_s.at[i], w3_r.at[i], sib)
    from_z(3)
    hop_y(2)
    from_sib(7)
    left(7, 1)

    for i in range(4):
        arrived(wall.at[:, rows(place(2 * rem(h + 4 - i, 4) + 1 - k), W)], w3_s.at[i], w3_r.at[i])
    ts[...] = dot(wall[...], feat[...], NN).astype(BF16)
    for i in range(1, N):
        to = rem(r + i, N)
        send(ts.at[rows(to, 16)], tb.at[i], t_s.at[i], t_r.at[i], (to, c, d))

    scale = 1.0 / TOTAL

    def gram_partial(g, first, n):
        cols = featr[first * W : (first + n) * W, :]
        g["gs"][...] = (dot(feat[rows(1 - k, 512), :], cols, NT) * scale).astype(BF16)
        swap(g)
        g["gsum"][...] = dot(feat[rows(k, 512), :], cols, NT) * scale

    def swap(g):
        send(g["gs"], g["gr"], g["sem_s"].at[0], g["sem_r"].at[0], sib)

    hp, hm, ho = rem(h + 1, 4), rem(h + 3, 4), rem(h + 2, 4)
    up, down = (r, c, 2 * hp + k), (r, c, 2 * hm + k)

    def step_one(g):
        arrived(g["gr"], g["sem_s"].at[0], g["sem_r"].at[0])
        g["gsum"][...] = g["gsum"][...] + g["gr"][...].astype(F32)
        g["gb16"][...] = g["gsum"][...].astype(BF16)
        for n, (name, i, at, core, dev) in enumerate(
            (
                ("ra", 0, ho, 0, up),
                ("ra", 1, ho, 1, down),
                ("rb", 0, hp, 1, up),
                ("rb", 1, hm, 0, down),
            )
        ):
            send(g["gb16"].at[half(at, core)], g[name].at[i], g["sem_s"].at[1 + n], g["sem_r"].at[1 + n], dev)

    def step_two(g):
        for i, (at, dev) in enumerate(((hp, up), (hm, down))):
            arrived(g["ra"].at[i], g["sem_s"].at[1 + i], g["sem_r"].at[1 + i])
            g["cs"][i] = (g["gsum"][half(at, i), :] + g["ra"][i].astype(F32)).astype(BF16)
            send(g["cs"].at[i], g["rc"].at[i], g["sem_s"].at[5 + i], g["sem_r"].at[5 + i], dev)

    def step_three(g):
        for i in range(2):
            arrived(g["rb"].at[i], g["sem_s"].at[3 + i], g["sem_r"].at[3 + i])
            arrived(g["rc"].at[i], g["sem_s"].at[5 + i], g["sem_r"].at[5 + i])
        upper = g["gsum"][half(h, 0), :] + g["rc"][0].astype(F32) + g["rb"][1].astype(F32)
        lower = g["gsum"][half(h, 1), :] + g["rb"][0].astype(F32) + g["rc"][1].astype(F32)
        return jnp.concatenate([upper, lower], axis=0)

    def hand_out(g, first, n):
        total = step_three(g)
        for i in range(first, first + n):
            block = total[:, (i - first) * W : (i - first + 1) * W]
            xb[i] = block.astype(BF16)
            to = rem(r + i, N)

            @pl.when(to != c)
            def _():
                copy(xb.at[i], gb.at[c], o_s.at[i], o_r.at[c], (r, to, d)).start()

            @pl.when(to == c)
            def _():
                gb[c] = xb[i]

            if 0 < i < ND - 1:
                xt[i - 1] = block.T.astype(BF16)
                send(xt.at[i - 1], xr.at[i - 1], v_s.at[i - 1], v_r.at[i - 1], (to, c, d))

    def relay(i):
        arrived(xr.at[i - 1], v_s.at[i - 1], v_r.at[i - 1])
        to = rem(r + N - i, N)
        stays = jnp.logical_and(to == c, d == c)

        @pl.when(jnp.logical_not(stays))
        def _():
            copy(xr.at[i - 1], gb.at[d], b_s.at[i - 1], o_r.at[d], (r, to, c)).start()

        @pl.when(stays)
        def _():
            gb[d] = xr[i - 1]

    sib_y(0, 1)
    right(0, 2)
    gram_partial(groups[0], 0, 3)
    step_one(groups[0])
    hop_y(3)

    sib_y(2, 3)
    right(2, 2)
    step_two(groups[0])
    total = ts[rows(r, 16), :].astype(F32)
    for i in range(1, N):
        arrived(tb.at[i], t_s.at[i], t_r.at[i])
        total = total + tb[i].astype(F32)
    strip = st.at[rows(r, 16)]
    st[rows(r, 16), :] = total.astype(BF16)
    for i in range(1, N):
        send(strip, strip, a_s.at[i], a_r.at[i], (rem(r + i, N), c, d))

    gram_partial(groups[1], 3, 2)
    step_one(groups[1])

    loads[3].wait()
    cls = lax.broadcasted_iota(jnp.int32, (W, ROWS), 0)
    onehot = jnp.where(l_ref[...] == cls + c * CLS, 1.0, 0.0).astype(BF16)
    own_f = feat[...].astype(F32)
    diag = jnp.sum(own_f * own_f, axis=1, keepdims=True)
    lane_u = lax.broadcasted_iota(jnp.int32, (N * W, W), 1)
    ulab[...] = jnp.where(lane_u == CLS, diag, -C * dot(feat[...], onehot, NT)) * scale
    step_two(groups[1])
    hand_out(groups[0], 0, 3)

    for i in range(1, N):
        arrived(st.at[rows(rem(r + N - i, N), 16)], a_s.at[i], a_r.at[i])
    ulab[...] = jnp.where(lane_u == CLS, 0.0, dot(feat[...], st[...], NT) * scale) + ulab[...]
    g = groups[2]
    g["gs"][...] = ulab[rows(1 - k, 512), :].astype(BF16)
    swap(g)
    g["gsum"][...] = ulab[rows(k, 512), :]
    arrived(g["gr"], g["sem_s"].at[0], g["sem_r"].at[0])
    g["gsum"][...] = g["gsum"][...] + g["gr"][...].astype(F32)
    g["gb16"][...] = g["gsum"][...].astype(BF16)
    for i in range(1, 4):
        to = rem(h + i, 4)
        send(g["gb16"].at[rows(to, W)], uq.at[i - 1], g["sem_s"].at[i], g["sem_r"].at[i], (r, c, 2 * to + k))
    hand_out(groups[1], 3, 2)
    relay(1)
    relay(2)

    delta = rem(c - r + N, N)
    eye = lax.broadcasted_iota(jnp.int32, (W, W), 0) == lane

    total = g["gsum"][rows(h, W), :]
    for i in range(1, 4):
        arrived(uq.at[i - 1], g["sem_s"].at[i], g["sem_r"].at[i])
        total = total + uq[i - 1].astype(F32)
    first = total.astype(BF16).astype(F32)
    second = (total - first)[:, CLS : CLS + 1]
    us[...] = jnp.where(lane == CLS + 1, second, total).astype(BF16)

    @pl.when(r != c)
    def _():
        copy(us, ub, u_s.at[0], u_r.at[0], flipped).start()

    @pl.when(r == c)
    def _():
        ub[...] = us[...]

    relay(3)
    for i in range(N):

        @pl.when(jnp.where(delta < ND, i != c, jnp.logical_or(c != d, i != d)))
        def _():
            arrived(gb.at[i], o_s.at[0], o_r.at[i])

        ridge = jnp.where(jnp.logical_and(eye, jnp.logical_and(r == c, d == i)), RIDGE, 0.0)
        gram_ref[:, i * W : (i + 1) * W] = gb[i].astype(F32) + ridge

    @pl.when(r != c)
    def _():
        arrived(ub, u_s.at[0], u_r.at[0])

    grad = ub[...].astype(F32)
    old = wpad[...]
    diag = grad[:, CLS : CLS + 1] + grad[:, CLS + 1 : CLS + 2] + RIDGE
    new = old - STEP_RATE * (grad + RIDGE * old) / diag
    new_ref[...] = new[:, :CLS]

    for m in sends:
        m.wait_send()

    @pl.when(r != c)
    def _():
        copy(wown, wown, w1_s.at[0], w1_r.at[0], sib).wait_send()
        copy(us, us, u_s.at[0], u_r.at[0], sib).wait_send()

    for i in range(ND):

        @pl.when(rem(r + i, N) != c)
        def _():
            copy(xb.at[i], xb.at[i], o_s.at[i], o_r.at[0], sib).wait_send()

    for i in range(1, ND - 1):

        @pl.when(jnp.logical_not(jnp.logical_and(rem(r + N - i, N) == c, d == c)))
        def _():
            copy(xr.at[0], xr.at[0], b_s.at[i - 1], o_r.at[0], sib).wait_send()


def shards(embeds, frequencies, phases, labels, weights):
    hbm = pl.BlockSpec(memory_space=pl.ANY)
    vmem = pl.BlockSpec(memory_space=pltpu.VMEM)
    buffers = [
        ((ROWS, DIN), BF16),
        ((DIN, W), BF16),
        ((1, W), F32),
        ((1, ROWS), jnp.int32),
        ((W, CLS), F32),
        ((N + ND - 1, 1, W), F32),
        ((W, W), F32),
        ((W, W), F32),
        ((N * W, DIN), BF16),
        (((ND - 1) * W, DIN), BF16),
        ((N * W, ROWS), BF16),
        ((ND * W, ROWS), BF16),
        ((W, W), F32),
        ((W, W), BF16),
        ((W, N * W), BF16),
        ((W, ROWS), BF16),
        ((N, 16, ROWS), BF16),
        ((W, ROWS), BF16),
        ((N * W, W), F32),
        ((ND, W, W), BF16),
        ((ND - 2, W, W), BF16),
        ((ND - 2, W, W), BF16),
        ((N, W, W), BF16),
        ((W, W), BF16),
        ((W, W), BF16),
        ((3, W, W), BF16),
    ]
    for dtype in (BF16, BF16, F32, BF16):
        buffers += [((4 * W, n), dtype) for n in GROUPS]
    for _ in range(4):
        buffers += [((2, HALF, n), BF16) for n in GROUPS]
    sem = lambda n: pltpu.SemaphoreType.DMA((n,))
    sems = [sem(7)] * (2 * len(GROUPS)) + [sem(5), sem(N + ND - 1), sem(N + ND - 1)]
    for n in (2, 2, 4, ND - 1, N, 4, 1, 4, 4, N, N, 1, ND - 2):
        sems += [sem(n), sem(n)]
    sems += [sem(ND), sem(N), sem(ND - 2)]
    return pl.pallas_call(
        kernel,
        out_shape=(
            jax.ShapeDtypeStruct((W, N * W), F32),
            jax.ShapeDtypeStruct((W, CLS), F32),
        ),
        in_specs=[hbm] * 5,
        out_specs=(vmem, vmem),
        scratch_shapes=[pltpu.VMEM(*b) for b in buffers] + sems,
        compiler_params=pltpu.CompilerParams(
            collective_id=0, has_side_effects=True, vmem_limit_bytes=56 * 2**20
        ),
    )(embeds, frequencies, phases.reshape(1, W), labels.reshape(1, ROWS), weights)


def solution(mesh):
    return jax.shard_map(
        shards,
        mesh=mesh,
        in_specs=(
            P("dp", None),
            P(None, ("trow", "tcol")),
            P(("trow", "tcol")),
            P("dp"),
            P(("tcol", "dp"), "trow"),
        ),
        out_specs=(P(("trow", "dp"), "tcol"), P(("tcol", "dp"), "trow")),
        check_vma=False,
    )
```
